128 devices in a mesh: dp: 16 (over x, z), tensor: 8 (over y, core).
Axes of the slice: x: 4, y: 4, z: 4, core: 2. Of those that a mesh axis runs over, the one named last changes fastest.
Arguments:
- activations: bfloat16 [16384, 6144], P('dp', 'tensor'), may hold values from -6 to 6
- out_grads: bfloat16 [16384, 6144], P(('dp', 'tensor')), may hold values from -0.1875 to 0.1875
- feedback: bfloat16 [16, 6144, 6144], P('dp', 'tensor'), may hold values from -6 to 6
- right_basis: float32 [6144, 32], replicated, may hold values from -0.078125 to 0.078125
Outputs:
- new_feedback: bfloat16 [16, 6144, 6144], P('dp', 'tensor')
- new_right: float32 [6144, 32], replicated
The draws below stay inside these ranges and needn't reach their ends.
All inputs are finite; a program needn't handle non-finite values.
Results may differ from the reference program's by a relative error of at most 0.013.
Values may be sent and summed in bfloat16 or wider, within the bound.
A program may use at most 128 MiB of HBM per device.

```python
import jax
import jax.numpy as jnp
from jax import lax

D = 6144
RANK = 32
TOK_DEV = 128
TOKENS = 1024
ALL_TOKENS = 16384
N_DP = 16
N_TENSOR = 8


def block_levels(stream_key, dims, cuts, least, top_value):
    loudness, own = 1.0, jax.random.fold_in(stream_key, 6)
    for axis_at, blocks in cuts:
        draws = jnp.exp(jax.random.uniform(jax.random.fold_in(own, axis_at), (blocks,), jnp.float32, least / len(cuts), top_value / len(cuts)))
        loudness = loudness * jnp.repeat(draws, dims[axis_at] // blocks).reshape([-1 if axis == axis_at else 1 for axis in range(len(dims))])
    return loudness


def normal_values(stream_key, dims, scale, bound, cuts=(), kind=jnp.bfloat16):
    result = scale * jax.random.normal(stream_key, dims, jnp.float32)
    if cuts:
        result = result * block_levels(stream_key, dims, cuts, -0.22, 0.18)
    return jnp.clip(result, -bound, bound).astype(kind)


def setup_inputs(seed: int = 0) -> dict:
    key_of = jax.random.split(jax.random.key(seed), 5)
    activations = normal_values(key_of[0], (ALL_TOKENS, D), 1.0, 6.0, ((0, 16), (1, 8)))
    out_grads = normal_values(key_of[1], (ALL_TOKENS, D), (1.0 / (TOK_DEV * N_TENSOR) ** 0.5), 0.1875, ((0, 128),))
    feedback = normal_values(key_of[2], (N_DP, D, D), 1.0, 6.0, ((0, 16), (1, 8)))
    right_basis = normal_values(key_of[3], (D, RANK), D ** -0.5, 0.078125, (), jnp.float32)
    return dict(activations=activations, out_grads=out_grads, feedback=feedback, right_basis=right_basis)


def reference(activations, out_grads, feedback, right_basis):
    highest = lax.Precision.HIGHEST
    inputs = activations.reshape(N_DP, TOKENS, D)
    cotangents = out_grads.reshape(N_DP, TOKENS, D)

    def left_term(items):
        inp, cot, carried = items
        projected = jnp.dot(cot.astype(jnp.float32), right_basis, precision=highest)
        first = jnp.dot(inp.astype(jnp.float32).T, projected, precision=highest)
        return first + jnp.dot(carried.astype(jnp.float32), right_basis, precision=highest)
    left = jnp.sum(lax.map(left_term, (inputs, cotangents, feedback)), axis=0)
    gram_matrix = jnp.dot(left.T, left, precision=highest)
    factor = jnp.linalg.cholesky(gram_matrix)
    left_basis = jax.scipy.linalg.solve_triangular(factor, left.T, lower=True).T

    def right_term(items):
        inp, cot, carried = items
        mapped = jnp.dot(inp.astype(jnp.float32), left_basis, precision=highest)
        first = jnp.dot(cot.astype(jnp.float32).T, mapped, precision=highest)
        return first + jnp.dot(carried.astype(jnp.float32).T, left_basis, precision=highest)
    new_right = jnp.sum(lax.map(right_term, (inputs, cotangents, feedback)), axis=0) / N_DP

    def error_term(items):
        inp, cot, carried = items
        merged = jnp.dot(inp.T.astype(jnp.float32), cot.astype(jnp.float32), preferred_element_type=jnp.float32) + carried.astype(jnp.float32)
        return (merged - jnp.dot(left_basis, new_right.T, precision=highest)).astype(jnp.bfloat16)
    new_feedback = lax.map(error_term, (inputs, cotangents, feedback))
    return (new_feedback, new_right)
```

```python
import functools

import jax
import jax.numpy as jnp
from jax import lax
from jax.experimental import pallas as pl
from jax.experimental.pallas import tpu as pltpu
from jax.sharding import PartitionSpec as P

MESH = pl.DeviceIdType.MESH
F32 = jnp.float32
BF16 = jnp.bfloat16
HIGHEST = lax.Precision.HIGHEST
RANK = 32
NY = 4
NT = 8
CHUNKS = 12
ROWS_FIRST = (((1,), (0,)), ((), ()))
ROWS_BOTH = (((1,), (1,)), ((), ()))


def dot(a, b, dims=ROWS_FIRST, precision=None):
    return lax.dot_general(a, b, dims, precision=precision, preferred_element_type=F32)


def split2(x):
    high = x.astype(BF16)
    low = (x - high.astype(F32)).astype(BF16)
    return high, low


def inverse_factor(gram):
    row = lax.broadcasted_iota(jnp.int32, (RANK, 128), 0)
    lane = lax.broadcasted_iota(jnp.int32, (RANK, 128), 1)
    work = jnp.where(lane < RANK, gram, jnp.where(lane == row + RANK, 1.0, 0.0))
    for k in range(RANK):
        column = jnp.broadcast_to(work[:, k : k + 1], (RANK, 128))
        pivot = column[k : k + 1, :]
        inv = lax.rsqrt(pivot)
        inv = inv * (1.5 - 0.5 * pivot * inv * inv)
        scaled = work[k : k + 1, :] * inv
        factor = jnp.where(row > k, column * inv, 0.0)
        work = jnp.where(row == k, scaled, work - factor * scaled)
    return work[:, RANK : 2 * RANK]


def chain_kernel(
    nx, nz,
    a_hbm, g_hbm, f_hbm, q_hbm,
    merged, p3, right,
    a_v, at_v, g_v, f_v, q_v, q2_v, gq_s, fq_v,
    la1, lb1, la2, lb2, left_v, left2_v,
    al_send, al_s, al2_v, linv_v,
    z_v, zsib, rs_s, y_s, zf,
    load_sem, dir_r, rel_r, sib_r, own_r, gq_r, l1_r, l2_r, al_r, zs_r, rs_r, y_r, ag_r, zf_r, send_sem,
):
    tok, d = g_hbm.shape
    feat = f_hbm.shape[0]
    half = d // 2
    piece_r, piece_c = RANK // nx, half // nz
    cw = d // CHUNKS
    dp, t = lax.axis_index("dp"), lax.axis_index("tensor")
    x, z = dp // nz, dp % nz
    y, c = t // 2, t % 2
    yp, ym, y2 = (y + 1) % NY, (y + 3) % NY, (y + 2) % NY
    sib = (dp, y * 2 + 1 - c)

    def at_y(yy):
        return (dp, yy * 2 + c)

    def rows(tt, first=0, count=None):
        return pl.ds(pl.multiple_of(tt * tok + first, 16), tok if count is None else count)

    def cols(j):
        return pl.ds(j * cw, cw)

    def remote(src, dst, send, recv, device):
        return pltpu.make_async_remote_copy(
            src_ref=src, dst_ref=dst, send_sem=send, recv_sem=recv, device_id=device, device_id_type=MESH
        )

    dp_peers = [
        (((x + i) % nx), ((z + k) % nz)) for i in range(nx) for k in range(nz) if i or k
    ]
    t_peers = [(t + k) % NT for k in range(1, NT)]

    g_load = pltpu.make_async_copy(g_hbm, g_v.at[rows(t), :], load_sem.at[0])
    q_load = pltpu.make_async_copy(q_hbm, q_v, load_sem.at[1])
    f_load = pltpu.make_async_copy(f_hbm, f_v, load_sem.at[2])
    a_load = pltpu.make_async_copy(a_hbm, a_v, load_sem.at[3])
    g_load.start()
    q_load.start()
    f_load.start()
    a_load.start()

    barrier = pltpu.get_barrier_semaphore()
    for tt in t_peers:
        pl.semaphore_signal(barrier, 1, device_id=(dp, tt), device_id_type=MESH)
    for xx, zz in dp_peers:
        pl.semaphore_signal(barrier, 1, device_id=(xx * nz + zz, t), device_id_type=MESH)
    q_load.wait()
    q_high, q_low = split2(q_v[...])
    q2_v[...] = jnp.concatenate([q_high, q_low], axis=0)
    g_load.wait()
    pl.semaphore_wait(barrier, len(t_peers) + len(dp_peers))

    def own_to_sib():
        return remote(g_v.at[rows(t), :], g_v.at[rows(t), :], send_sem.at[0], own_r, sib)

    def own_from_sib():
        block = g_v.at[rows(sib[1]), :]
        return remote(block, block, send_sem.at[0], own_r, sib)

    def send_dir(j):
        block = g_v.at[rows(t), cols(j)]
        remote(block, block, send_sem.at[1], dir_r.at[2 * j], at_y(yp)).start()
        remote(block, block, send_sem.at[2], dir_r.at[2 * j + 1], at_y(ym)).start()

    def fwd(tt, j, k):
        block = g_v.at[rows(tt), cols(j)]
        remote(block, block, send_sem.at[3 + k], sib_r.at[3 * j + k], sib).start()

    def take(tt, j, sem, first=0, count=None):
        block = g_v.at[rows(tt, first, count), cols(j)]
        remote(block, block, send_sem.at[0], sem, sib).wait_recv()

    def relay(j):
        take(ym * 2 + c, j, dir_r.at[2 * j])
        block = g_v.at[rows(ym * 2 + c, 0, tok // 2), cols(j)]
        remote(block, block, send_sem.at[6], rel_r.at[2 * j], at_y(yp)).start()
        take(yp * 2 + c, j, dir_r.at[2 * j + 1])
        block = g_v.at[rows(yp * 2 + c, tok // 2, tok // 2), cols(j)]
        remote(block, block, send_sem.at[7], rel_r.at[2 * j + 1], at_y(ym)).start()

    def opposite(j):
        take(y2 * 2 + c, j, rel_r.at[2 * j], 0, tok // 2)
        take(y2 * 2 + c, j, rel_r.at[2 * j + 1], tok // 2, tok // 2)
        fwd(y2 * 2 + c, j, 2)

    def pump(j):
        relay(j)
        if j + 2 < CHUNKS:
            send_dir(j + 2)
        fwd(ym * 2 + c, j, 0)
        fwd(yp * 2 + c, j, 1)
        if j >= 2:
            opposite(j - 2)

    def merge(j):
        if j == 0:
            own_from_sib().wait_recv()
        take(ym * 2 + 1 - c, j, sib_r.at[3 * j])
        take(yp * 2 + 1 - c, j, sib_r.at[3 * j + 1])
        take(y2 * 2 + 1 - c, j, sib_r.at[3 * j + 2])
        width = min(256, cw)

        def step(i, carry):
            at = pl.ds(pl.multiple_of(j * cw + i * width, 128), width)
            merged[:, at] = dot(at_v[...], g_v[:, at]) + f_v[:, at].astype(F32)
            return carry

        lax.fori_loop(0, cw // width, step, 0)

    own_to_sib().start()
    send_dir(0)

    gq2 = dot(q2_v[...], g_v[rows(t), :], ROWS_BOTH)
    gq_s[t] = gq2[:RANK] + gq2[RANK:]
    for tt in t_peers:
        remote(gq_s.at[t], gq_s.at[t], send_sem.at[8], gq_r.at[t], (dp, tt)).start()
    send_dir(1)

    f_load.wait()
    depth = d // 3
    for k in range(d // depth):
        at = pl.ds(k * depth, depth)
        part = dot(f_v[:, at], q2_v[:, at], ROWS_BOTH)
        if k == 0:
            fq_v[...] = part
        else:
            fq_v[...] += part
    a_load.wait()
    for k in range(NT):
        at_v[:, k * tok : (k + 1) * tok] = jnp.transpose(a_v[k * tok : (k + 1) * tok, :])
    pump(0)

    for tt in t_peers:
        remote(gq_s.at[tt], gq_s.at[tt], send_sem.at[8], gq_r.at[tt], sib).wait_recv()
    gq = jnp.concatenate([gq_s[k] for k in range(NT)], axis=1)
    part = dot(jnp.concatenate(split2(gq), axis=0), a_v[...])
    fq = fq_v[...]
    left_part = part[:RANK] + part[RANK:] + jnp.transpose(fq[:, :RANK] + fq[:, RANK:])

    hr = RANK // 2
    la1[x] = left_part[:hr].astype(BF16)
    lb1[z] = left_part[hr:].astype(BF16)

    def x_peers():
        return [((x + i) % nx) for i in range(1, nx)]

    def z_peers():
        return [((z + i) % nz) for i in range(1, nz)]

    def left_stage(slots_x, slots_z, sems, sem_at, start):
        for xx in x_peers():
            if start:
                remote(slots_x.at[x], slots_x.at[x], send_sem.at[sem_at], sems.at[x], (xx * nz + z, t)).start()
            else:
                remote(slots_x.at[xx], slots_x.at[xx], send_sem.at[sem_at], sems.at[xx], sib).wait_recv()
        for zz in z_peers():
            if start:
                remote(slots_z.at[z], slots_z.at[z], send_sem.at[sem_at + 1], sems.at[nx + z], (x * nz + zz, t)).start()
            else:
                remote(slots_z.at[zz], slots_z.at[zz], send_sem.at[sem_at + 1], sems.at[nx + zz], sib).wait_recv()

    def total(slots, n):
        out = slots[0].astype(F32)
        for k in range(1, n):
            out = out + slots[k].astype(F32)
        return out

    left_stage(la1, lb1, l1_r, 9, True)
    pump(1)
    left_stage(la1, lb1, l1_r, 9, False)
    la2[z] = total(la1, nx).astype(BF16)
    lb2[x] = total(lb1, nz).astype(BF16)
    left_stage(lb2, la2, l2_r, 11, True)
    pump(2)
    left_stage(lb2, la2, l2_r, 11, False)
    left_v[:hr] = total(la2, nz)
    left_v[hr:] = total(lb2, nx)
    left = left_v[...]
    left2_v[...] = jnp.concatenate(split2(left), axis=0)

    al = dot(left2_v[...], at_v[...])
    al = al[:RANK] + al[RANK:]
    gram = jnp.concatenate(
        [dot(left, left, ROWS_BOTH, HIGHEST), jnp.zeros((RANK, 128 - RANK), F32)], axis=1
    )
    for k in range(NT):
        al_send[k, :RANK] = al[:, k * tok : (k + 1) * tok]
        al_send[k, RANK:] = gram
    pump(3)
    for tt in t_peers:
        remote(al_send.at[tt], al_s.at[t], send_sem.at[13], al_r.at[t], (dp, tt)).start()
    al_s[t] = al_send[t]

    zw = min(512, d)

    def z_first(i, carry):
        at = pl.ds(pl.multiple_of(i * zw, 128), zw)
        r = dot(left2_v[...], f_v[:, at])
        z_v[:, at] = r[:RANK] + r[RANK:]
        return carry

    lax.fori_loop(0, d // zw, z_first, 0)
    pump(4)
    for tt in t_peers:
        remote(al_s.at[tt], al_s.at[tt], send_sem.at[13], al_r.at[tt], sib).wait_recv()
    al_sum = total(al_s, NT)
    al2_v[...] = jnp.concatenate(split2(al_sum[:RANK]), axis=0)
    linv_v[...] = jnp.concatenate([al_sum[RANK:], al_sum[RANK:]], axis=0)[:RANK]

    hw = min(512, half)

    def z_second(base):
        def step(i, carry):
            at = pl.ds(pl.multiple_of(base + i * hw, 128), hw)
            r = dot(al2_v[...], g_v[rows(t), at])
            z_v[:, at] += r[:RANK] + r[RANK:]
            return carry

        lax.fori_loop(0, half // hw, step, 0)

    mine, other = c * half, (1 - c) * half
    my_half = pl.ds(pl.multiple_of(mine, 128), half)
    sib_half = pl.ds(pl.multiple_of(other, 128), half)
    z_second(other)
    remote(z_v.at[:, sib_half], zsib, send_sem.at[14], zs_r, sib).start()
    z_second(mine)
    pump(5)
    remote(zsib, zsib, send_sem.at[14], zs_r, sib).wait_recv()
    z_v[:, my_half] += zsib[...]

    def piece(xx, zz):
        return (
            pl.ds(pl.multiple_of(xx * piece_r, 8), piece_r),
            pl.ds(pl.multiple_of(mine + zz * piece_c, 128), piece_c),
        )

    for xx, zz in dp_peers:
        remote(z_v.at[piece(xx, zz)], rs_s.at[dp], send_sem.at[15], rs_r.at[dp], (xx * nz + zz, t)).start()
    rs_s[dp] = z_v[piece(x, z)]
    linv = inverse_factor(linv_v[...])
    linv_v[:, :RANK] = linv
    left = left_v[...]
    p_high, p_low = split2(dot(linv, left, precision=HIGHEST))
    p_rows = jnp.concatenate([p_high, p_high, p_low, jnp.zeros((RANK, feat), BF16)], axis=0)
    p3[...] = jnp.transpose(p_rows.astype(F32)).astype(BF16)
    pump(6)
    merge(0)
    merge(1)
    for xx, zz in dp_peers:
        src = xx * nz + zz
        remote(rs_s.at[src], rs_s.at[src], send_sem.at[15], rs_r.at[src], sib).wait_recv()
    y_s[y] = total(rs_s, nx * nz)
    for yy in (yp, y2, ym):
        remote(y_s.at[y], y_s.at[y], send_sem.at[16], y_r.at[y], at_y(yy)).start()
    pump(7)
    merge(2)
    merge(3)
    for yy in (yp, y2, ym):
        remote(y_s.at[yy], y_s.at[yy], send_sem.at[16], y_r.at[yy], sib).wait_recv()
    zf[piece(x, z)] = total(y_s, NY)
    for xx, zz in dp_peers:
        remote(zf.at[piece(x, z)], zf.at[piece(x, z)], send_sem.at[17], ag_r.at[dp], (xx * nz + zz, t)).start()
    pump(8)
    merge(4)
    merge(5)
    pump(9)
    merge(6)
    merge(7)
    for xx, zz in dp_peers:
        src = xx * nz + zz
        remote(zf.at[piece(xx, zz)], zf.at[piece(xx, zz)], send_sem.at[17], ag_r.at[src], sib).wait_recv()
    remote(zf.at[:, my_half], zf.at[:, my_half], send_sem.at[18], zf_r, sib).start()
    pump(10)
    merge(8)
    remote(zf.at[:, sib_half], zf.at[:, sib_half], send_sem.at[18], zf_r, sib).wait_recv()
    linv = linv_v[:, :RANK]

    def finish(i, carry):
        at = pl.ds(pl.multiple_of(i * zw, 128), zw)
        right[:, at] = dot(linv, zf[:, at], precision=HIGHEST) * (1.0 / (nx * nz))
        return carry

    lax.fori_loop(0, d // zw, finish, 0)
    pump(11)
    merge(9)
    opposite(CHUNKS - 2)
    opposite(CHUNKS - 1)
    merge(10)
    merge(11)

    def sent(ref, sem):
        remote(ref, ref, send_sem.at[sem], own_r, sib).wait_send()

    own = g_v.at[rows(t), :]
    for k in range(6):
        sent(own, k)
    sent(g_v.at[rows(t, 0, tok // 2), :], 6)
    sent(g_v.at[rows(t, 0, tok // 2), :], 7)
    sent(gq_s.at[pl.ds(0, NT - 1)], 8)
    if nx > 1:
        sent(la1.at[pl.ds(0, nx - 1)], 9)
        sent(lb2.at[pl.ds(0, nx - 1)], 11)
    if nz > 1:
        sent(lb1.at[pl.ds(0, nz - 1)], 10)
        sent(la2.at[pl.ds(0, nz - 1)], 12)
    sent(al_s.at[pl.ds(0, NT - 1)], 13)
    sent(zsib, 14)
    sent(rs_s.at[pl.ds(0, nx * nz - 1)], 15)
    sent(y_s.at[pl.ds(0, NY - 1)], 16)
    sent(rs_s.at[pl.ds(0, nx * nz - 1)], 17)
    sent(zsib, 18)


def update_kernel(merged, p3, right, out, right_out, stage, r3_v, sems, right_sem):
    d = merged.shape[1]
    width = stage.shape[2]
    steps = d // width
    right_copy = pltpu.make_async_copy(right, right_out, right_sem)
    right_copy.start()

    def block(i):
        return pl.ds(pl.multiple_of(i * width, 128), width)

    def copy(i):
        return pltpu.make_async_copy(stage.at[i % 2], out.at[:, block(i)], sems.at[i % 2])

    for i in range(steps):
        r_high, r_low = split2(right[:, block(i)])
        r3_v[...] = jnp.concatenate([r_high, r_low, r_high, jnp.zeros((RANK, width), BF16)], axis=0)
        if i >= 2:
            copy(i - 2).wait()
        stage[i % 2] = (merged[:, block(i)] - dot(p3[...], r3_v[...])).astype(BF16)
        copy(i).start()
    copy(steps - 2).wait()
    copy(steps - 1).wait()
    right_copy.wait()


def body(nx, nz, activations, out_grads, feedback, right_basis):
    tokens, feat = activations.shape
    tok, d = out_grads.shape
    half = d // 2
    piece = (RANK // nx, half // nz)
    any_spec = pl.BlockSpec(memory_space=pl.ANY)
    vmem_spec = pl.BlockSpec(memory_space=pltpu.VMEM)
    dma = pltpu.SemaphoreType.DMA
    merged, p3, right = pl.pallas_call(
        functools.partial(chain_kernel, nx, nz),
        out_shape=(
            pltpu.VMEM((feat, d), F32),
            pltpu.VMEM((feat, 128), BF16),
            pltpu.VMEM((RANK, d), F32),
        ),
        in_specs=[any_spec] * 4,
        out_specs=(vmem_spec,) * 3,
        scratch_shapes=[
            pltpu.VMEM((tokens, feat), BF16),
            pltpu.VMEM((feat, tokens), BF16),
            pltpu.VMEM((tokens, d), BF16),
            pltpu.VMEM((feat, d), BF16),
            pltpu.VMEM((RANK, d), F32),
            pltpu.VMEM((2 * RANK, d), BF16),
            pltpu.VMEM((NT, RANK, tok), F32),
            pltpu.VMEM((feat, 2 * RANK), F32),
            pltpu.VMEM((nx, RANK // 2, feat), BF16),
            pltpu.VMEM((nz, RANK // 2, feat), BF16),
            pltpu.VMEM((nz, RANK // 2, feat), BF16),
            pltpu.VMEM((nx, RANK // 2, feat), BF16),
            pltpu.VMEM((RANK, feat), F32),
            pltpu.VMEM((2 * RANK, feat), BF16),
            pltpu.VMEM((NT, 2 * RANK, tok), F32),
            pltpu.VMEM((NT, 2 * RANK, tok), F32),
            pltpu.VMEM((2 * RANK, tok), BF16),
            pltpu.VMEM((RANK, 128), F32),
            pltpu.VMEM((RANK, d), F32),
            pltpu.VMEM((RANK, half), F32),
            pltpu.VMEM((nx * nz,) + piece, F32),
            pltpu.VMEM((NY,) + piece, F32),
            pltpu.VMEM((RANK, d), F32),
            dma((4,)),
            dma((2 * CHUNKS,)),
            dma((2 * CHUNKS,)),
            dma((3 * CHUNKS,)),
            dma,
            dma((NT,)),
            dma((nx + nz,)),
            dma((nx + nz,)),
            dma((NT,)),
            dma,
            dma((nx * nz,)),
            dma((NY,)),
            dma((nx * nz,)),
            dma,
            dma((19,)),
        ],
        compiler_params=pltpu.CompilerParams(
            collective_id=0, has_side_effects=True, vmem_limit_bytes=VMEM_LIMIT
        ),
        name="gather_and_factors",
    )(activations, out_grads, feedback[0], right_basis.T)
    width = min(512, d // 2)
    vmem = functools.partial(pltpu.with_memory_space_constraint, memory_space=pltpu.VMEM)
    new_feedback, new_right = pl.pallas_call(
        update_kernel,
        out_shape=(
            jax.ShapeDtypeStruct((feat, d), BF16),
            jax.ShapeDtypeStruct((RANK, d), F32),
        ),
        in_specs=[vmem_spec] * 3,
        out_specs=(any_spec, any_spec),
        scratch_shapes=[
            pltpu.VMEM((2, feat, width), BF16),
            pltpu.VMEM((128, width), BF16),
            dma((2,)),
            dma,
        ],
        compiler_params=pltpu.CompilerParams(vmem_limit_bytes=8 << 20),
        name="update",
    )(vmem(merged), vmem(p3), vmem(right))
    return new_feedback[None], new_right.T


VMEM_LIMIT = 40 << 20


def solution(mesh):
    nx = nz = 4
    in_specs = (P("dp", "tensor"), P(("dp", "tensor"), None), P("dp", "tensor", None), P())
    out_specs = (P("dp", "tensor", None), P())
    return jax.shard_map(
        functools.partial(body, nx, nz), mesh=mesh, in_specs=in_specs, out_specs=out_specs, check_vma=False
    )
```

```python
import functools

import jax
import jax.numpy as jnp
from jax import lax
from jax.experimental import pallas as pl
from jax.experimental.pallas import tpu as pltpu
from jax.sharding import PartitionSpec as P

MESH = pl.DeviceIdType.MESH
F32 = jnp.float32
BF16 = jnp.bfloat16
HIGHEST = lax.Precision.HIGHEST
RANK = 32
NY = 4
NT = 8
WIDTHS = (256,) + (512,) * 11 + (256,)
STARTS = tuple(sum(WIDTHS[:k]) for k in range(len(WIDTHS)))
CHUNKS = len(WIDTHS)
ROWS_FIRST = (((1,), (0,)), ((), ()))
ROWS_BOTH = (((1,), (1,)), ((), ()))


def dot(a, b, dims=ROWS_FIRST, precision=None):
    return lax.dot_general(a, b, dims, precision=precision, preferred_element_type=F32)


def split2(x):
    high = x.astype(BF16)
    low = (x - high.astype(F32)).astype(BF16)
    return high, low


def split3(x):
    high, low = split2(x)
    return high, low, (x - high.astype(F32) - low.astype(F32)).astype(BF16)


def inverse_factor(gram):
    row = lax.broadcasted_iota(jnp.int32, (RANK, 128), 0)
    lane = lax.broadcasted_iota(jnp.int32, (RANK, 128), 1)
    work = jnp.where(lane < RANK, gram, jnp.where(lane == row + RANK, 1.0, 0.0))
    for k in range(RANK):
        column = jnp.broadcast_to(work[:, k : k + 1], (RANK, 128))
        pivot = column[k : k + 1, :]
        inv = lax.rsqrt(pivot)
        inv = inv * (1.5 - 0.5 * pivot * inv * inv)
        scaled = work[k : k + 1, :] * inv
        factor = jnp.where(row > k, column * inv, 0.0)
        work = jnp.where(row == k, scaled, work - factor * scaled)
    return work[:, RANK : 2 * RANK]


def chain_kernel(
    nx, nz, plan,
    a_hbm, g_hbm, f_hbm, q_hbm,
    merged, p3, right,
    a_v, at_v, g_v, f_v, q_v, q2_v, gq_s, fq_v,
    la1, lb1, la2, lb2, left_v, left2_v,
    al_send, al_sib, al_s, al_fwd, al_in, al2_v, linv_v,
    z_v, zsib, rs_s, y_s, zf,
    load_sem, dir_r, rel_r, sib_r, own_r, gq_r, l1_r, l2_r, als_r, al_r, ali_r, zs_r, rs_r, y_r, ag_r, zf_r, send_sem, round_sem,
):
    tok, d = g_hbm.shape
    feat = f_hbm.shape[0]
    half = d // 2
    piece_r, piece_c = RANK // nx, half // nz
    zw = min(512, d)
    hw = min(512, half)
    hr = RANK // 2
    dp, t = lax.axis_index("dp"), lax.axis_index("tensor")
    x, z = dp // nz, dp % nz
    y, c = t // 2, t % 2
    yp, ym, y2 = (y + 1) % NY, (y + 3) % NY, (y + 2) % NY
    sib = (dp, y * 2 + 1 - c)
    mine, other = c * half, (1 - c) * half
    my_half = pl.ds(pl.multiple_of(mine, 128), half)
    sib_half = pl.ds(pl.multiple_of(other, 128), half)
    dp_peers = [(((x + i) % nx), ((z + k) % nz)) for i in range(nx) for k in range(nz) if i or k]
    x_peers = [((x + i) % nx) for i in range(1, nx)]
    z_peers = [((z + i) % nz) for i in range(1, nz)]
    outgoing = []

    def at_y(yy):
        return (dp, yy * 2 + c)

    def rows(tt, first=0, count=None):
        return pl.ds(pl.multiple_of(tt * tok + first, 16), tok if count is None else count)

    def cols(j):
        return pl.ds(STARTS[j], WIDTHS[j])

    def remote(src, dst, send, recv, device):
        return pltpu.make_async_remote_copy(
            src_ref=src, dst_ref=dst, send_sem=send, recv_sem=recv, device_id=device, device_id_type=MESH
        )

    def send(src, dst, sem, recv, device):
        remote(src, dst, send_sem.at[sem], recv, device).start()
        outgoing.append(sem)

    def receive(ref, recv):
        remote(ref, ref, send_sem.at[0], recv, sib).wait_recv()

    def piece(xx, zz):
        return (
            pl.ds(pl.multiple_of((xx + NY - y) % nx * piece_r, 8), piece_r),
            pl.ds(pl.multiple_of(mine + zz * piece_c, 128), piece_c),
        )

    def total(slots, n):
        out = slots[0].astype(F32)
        for k in range(1, n):
            out = out + slots[k].astype(F32)
        return out

    loads = [
        pltpu.make_async_copy(g_hbm, g_v.at[rows(t), :], load_sem.at[0]),
        pltpu.make_async_copy(q_hbm, q_v, load_sem.at[1]),
        pltpu.make_async_copy(f_hbm, f_v, load_sem.at[2]),
        pltpu.make_async_copy(a_hbm, a_v, load_sem.at[3]),
    ]

    near = [(dp, (y * 2 + c + 2) % NT), (dp, (y * 2 + c + 6) % NT)]
    near += [(((x + i) % nx) * nz + z, t) for i in (1, nx - 1)] + [(x * nz + (z + i) % nz, t) for i in (1, nz - 1)]

    def enter():
        loads[0].start()
        loads[1].start()
        barrier = pltpu.get_barrier_semaphore()
        for device in near + [sib]:
            pl.semaphore_signal(barrier, 1, device_id=device, device_id_type=MESH)
        loads[0].wait()
        loads[2].start()
        loads[3].start()
        loads[1].wait()
        q2_v[...] = jnp.concatenate(split2(q_v[...]), axis=0)
        pl.semaphore_wait(barrier, len(near) + 1)

    def tell(k):
        for device in near[2:] if k else near:
            pl.semaphore_signal(round_sem.at[k], 1, device_id=device, device_id_type=MESH)

    def hear(k):
        pl.semaphore_wait(round_sem.at[k], len(near[2:] if k else near))

    def wait_load(k):
        loads[k].wait()


    def own():
        send(g_v.at[rows(t), :], g_v.at[rows(t), :], 0, own_r, sib)

    def direct(j):
        block = g_v.at[rows(t), cols(j)]
        send(block, block, 1, dir_r.at[2 * j], at_y(yp))
        send(block, block, 2, dir_r.at[2 * j + 1], at_y(ym))

    def to_sib(tt, j, k):
        block = g_v.at[rows(tt), cols(j)]
        send(block, block, 3 + k, sib_r.at[3 * j + k], sib)

    def relay(j):
        receive(g_v.at[rows(ym * 2 + c), cols(j)], dir_r.at[2 * j])
        block = g_v.at[rows(ym * 2 + c, 0, tok // 2), cols(j)]
        send(block, block, 6, rel_r.at[2 * j], at_y(yp))
        receive(g_v.at[rows(yp * 2 + c), cols(j)], dir_r.at[2 * j + 1])
        block = g_v.at[rows(yp * 2 + c, tok // 2, tok // 2), cols(j)]
        send(block, block, 7, rel_r.at[2 * j + 1], at_y(ym))

    def cross(j):
        to_sib(ym * 2 + c, j, 0)
        to_sib(yp * 2 + c, j, 1)

    def opposite(j):
        receive(g_v.at[rows(y2 * 2 + c, 0, tok // 2), cols(j)], rel_r.at[2 * j])
        receive(g_v.at[rows(y2 * 2 + c, tok // 2, tok // 2), cols(j)], rel_r.at[2 * j + 1])
        to_sib(y2 * 2 + c, j, 2)

    def pump(j):
        relay(j)
        if j + 3 < CHUNKS:
            direct(j + 3)
        cross(j)
        if j >= 2:
            opposite(j - 2)

    def absorb(j):
        if j == 0:
            receive(g_v.at[rows(sib[1]), :], own_r)
        for k, yy in enumerate((ym, yp, y2)):
            receive(g_v.at[rows(yy * 2 + 1 - c), cols(j)], sib_r.at[3 * j + k])

    def merge(j):
        absorb(j)
        width = min(256, WIDTHS[j])

        def step(i, carry):
            at = pl.ds(pl.multiple_of(STARTS[j] + i * width, 128), width)
            merged[:, at] = dot(at_v[...], g_v[:, at]) + f_v[:, at].astype(F32)
            return carry

        lax.fori_loop(0, WIDTHS[j] // width, step, 0)


    y_peers = (yp, y2, ym)

    def project():
        gq2 = dot(q2_v[...], g_v[rows(t), :], ROWS_BOTH)
        gq_s[c, y] = gq2[:RANK] + gq2[RANK:]

    def project_send():
        for yy in y_peers:
            send(gq_s.at[c, y], gq_s.at[c, y], 8, gq_r.at[y], at_y(yy))
        send(gq_s.at[c, y], gq_s.at[c, y], 19, gq_r.at[NY + y], sib)

    def project_cross():
        for yy in y_peers:
            receive(gq_s.at[c, yy], gq_r.at[yy])
            send(gq_s.at[c, yy], gq_s.at[c, yy], 19, gq_r.at[NY + yy], sib)

    def carried():
        wait_load(2)
        depth = d // 3
        for k in range(d // depth):
            at = pl.ds(k * depth, depth)
            part = dot(f_v[:, at], q2_v[:, at], ROWS_BOTH)
            if k == 0:
                fq_v[...] = part
            else:
                fq_v[...] += part

    def flip():
        wait_load(3)
        for k in range(NT):
            at_v[:, k * tok : (k + 1) * tok] = jnp.transpose(a_v[k * tok : (k + 1) * tok, :])

    def left_start():
        for yy in range(NY):
            receive(gq_s.at[1 - c, yy], gq_r.at[NY + yy])
        gq = jnp.concatenate([gq_s[k % 2, k // 2] for k in range(NT)], axis=1)
        part = dot(jnp.concatenate(split2(gq), axis=0), a_v[...])
        fq = fq_v[...]
        left_part = part[:RANK] + part[RANK:] + jnp.transpose(fq[:, :RANK] + fq[:, RANK:])
        la1[x] = left_part[:hr].astype(BF16)
        lb1[z] = left_part[hr:].astype(BF16)
        left_send(la1, lb1, l1_r, 9)

    def left_send(slots_x, slots_z, sems, at):
        for xx in x_peers:
            send(slots_x.at[x], slots_x.at[x], at, sems.at[x], (xx * nz + z, t))
        for zz in z_peers:
            send(slots_z.at[z], slots_z.at[z], at + 1, sems.at[nx + z], (x * nz + zz, t))

    def left_receive(slots_x, slots_z, sems):
        for xx in x_peers:
            receive(slots_x.at[xx], sems.at[xx])
        for zz in z_peers:
            receive(slots_z.at[zz], sems.at[nx + zz])

    def left_second():
        left_receive(la1, lb1, l1_r)
        la2[z] = total(la1, nx).astype(BF16)
        lb2[x] = total(lb1, nz).astype(BF16)
        left_send(lb2, la2, l2_r, 11)

    def left_end():
        left_receive(lb2, la2, l2_r)
        left_v[:hr] = total(la2, nz)
        left_v[hr:] = total(lb2, nx)
        left2_v[...] = jnp.concatenate(split2(left_v[...]), axis=0)

    def mapped():
        left = left_v[...]
        al = dot(left2_v[...], at_v[...])
        al = al[:RANK] + al[RANK:]
        gram = dot(left, left, ROWS_BOTH, HIGHEST)
        gram = jnp.concatenate([gram[8 * k : 8 * k + 8] for k in range(RANK // 8)], axis=1)
        for k in range(NT):
            al_send[k % 2, k // 2, :RANK] = al[:, k * tok : (k + 1) * tok]
            al_send[k % 2, k // 2, RANK:] = gram
        send(al_send.at[1 - c], al_sib, 20, als_r, sib)

    def mapped_send():
        receive(al_sib, als_r)
        al_send[c] += al_sib[...]
        for yy in y_peers:
            send(al_send.at[c, yy], al_s.at[y], 13, al_r.at[y], (((x + 1) % nx) * nz + z, yy * 2 + c))

    def mapped_relay():
        for yy in y_peers:
            receive(al_s.at[yy], al_r.at[yy])
        al_s[y] = al_send[c, y]
        fwd = al_s[yp, :RANK] + al_s[y2, :RANK] + al_s[ym, :RANK]
        al_fwd[...] = fwd
        send(al_fwd, al_in, 21, ali_r, (((x + nx - 1) % nx) * nz + z, t))
        gram = total(al_s, NY)[RANK:]
        gram = jnp.concatenate([gram[:, RANK * k : RANK * (k + 1)] for k in range(RANK // 8)], axis=0)
        linv_v[...] = jnp.concatenate([gram, jnp.zeros((RANK, 128 - RANK), F32)], axis=1)

    def z_first():
        def step(i, carry):
            at = pl.ds(pl.multiple_of(i * zw, 128), zw)
            r = dot(left2_v[...], f_v[:, at])
            z_v[:, at] = r[:RANK] + r[RANK:]
            return carry

        lax.fori_loop(0, d // zw, step, 0)

    def mapped_end():
        receive(al_in, ali_r)
        al2_v[...] = jnp.concatenate(split2(al_send[c, y, :RANK] + al_in[...]), axis=0)

    def z_second(base):
        def step(i, carry):
            at = pl.ds(pl.multiple_of(base + i * hw, 128), hw)
            r = dot(al2_v[...], g_v[rows(t), at])
            z_v[:, at] += r[:RANK] + r[RANK:]
            return carry

        lax.fori_loop(0, half // hw, step, 0)

    def z_send():
        z_second(other)
        send(z_v.at[:, sib_half], zsib, 14, zs_r, sib)
        z_second(mine)

    def z_scatter():
        receive(zsib, zs_r)
        z_v[:, my_half] += zsib[...]
        for xx, zz in dp_peers:
            send(z_v.at[piece(xx, zz)], rs_s.at[dp], 15, rs_r.at[dp], (xx * nz + zz, t))
        rs_s[dp] = z_v[piece(x, z)]

    def factor():
        linv = inverse_factor(linv_v[...])
        linv_v[:, :RANK] = linv
        p_high, p_low = split2(dot(linv, left_v[...], precision=HIGHEST))
        p_rows = jnp.concatenate([p_high, p_high, p_low, jnp.zeros((RANK, feat), BF16)], axis=0)
        p3[...] = jnp.transpose(p_rows.astype(F32)).astype(BF16)

    def z_over_y():
        for xx, zz in dp_peers:
            receive(rs_s.at[xx * nz + zz], rs_r.at[xx * nz + zz])
        y_s[y] = total(rs_s, nx * nz)
        for yy in (yp, y2, ym):
            send(y_s.at[y], y_s.at[y], 16, y_r.at[y], (((x + NY - y + yy) % nx) * nz + z, yy * 2 + c))

    def z_back():
        for yy in (yp, y2, ym):
            receive(y_s.at[yy], y_r.at[yy])
        zf[piece(x, z)] = total(y_s, NY)
        for xx, zz in dp_peers:
            send(zf.at[piece(x, z)], zf.at[piece(x, z)], 17, ag_r.at[dp], (xx * nz + zz, t))

    def z_cross():
        for xx, zz in dp_peers:
            receive(zf.at[piece(xx, zz)], ag_r.at[xx * nz + zz])
        send(zf.at[:, my_half], zf.at[:, my_half], 18, zf_r, sib)

    def z_end():
        receive(zf.at[:, sib_half], zf_r)

    def finish():
        l1, l2, l3 = split3(linv_v[:, :RANK])
        lhs = jnp.concatenate([l1, l1, l2, l1, l2, l3], axis=1)

        def step(i, carry):
            at = pl.ds(pl.multiple_of(i * zw, 128), zw)
            z1, z2, z3 = split3(zf[:, at])
            rhs = jnp.concatenate([z1, z2, z1, z3, z2, z1], axis=0)
            right[:, at] = dot(lhs, rhs) * (1.0 / (nx * nz))
            return carry

        lax.fori_loop(0, d // zw, step, 0)

    def leave():
        gather = [g_v.at[rows(t), :]] * 6 + [g_v.at[rows(t, 0, tok // 2), :]] * 2
        pieces = gather + [gq_s.at[0, pl.ds(0, NY - 1)]]
        for slots in (la1, lb1, lb2, la2):
            pieces.append(slots.at[pl.ds(0, slots.shape[0] - 1)])
        pieces += [al_s.at[pl.ds(0, NY - 1)], zsib, rs_s.at[pl.ds(0, nx * nz - 1)]]
        pieces += [y_s.at[pl.ds(0, NY - 1)], rs_s.at[pl.ds(0, nx * nz - 1)], zsib]
        pieces += [gq_s.at[0], al_sib, al_in]
        for sem, ref in enumerate(pieces):
            if sem in outgoing:
                remote(ref, ref, send_sem.at[sem], own_r, sib).wait_send()

    steps = dict(tell=tell, hear=hear, project_send=project_send, project_cross=project_cross,
        enter=enter, wait_load=wait_load, absorb=absorb, own=own, direct=direct, relay=relay, cross=cross, opposite=opposite, pump=pump, merge=merge,
        project=project, carried=carried, flip=flip, left_start=left_start, left_second=left_second,
        left_end=left_end, mapped=mapped, mapped_send=mapped_send, mapped_relay=mapped_relay, z_first=z_first, mapped_end=mapped_end,
        z_send=z_send, z_scatter=z_scatter, factor=factor, z_over_y=z_over_y, z_back=z_back, z_cross=z_cross,
        z_end=z_end, finish=finish, leave=leave,
    )
    for name, *args in plan:
        steps[name](*args)


def chain_plan():
    return [
        ("enter",), ("tell", 0), ("direct", 0), ("project",), ("hear", 0), ("project_send",), ("direct", 1),
        ("direct", 2), ("tell", 1), ("carried",), ("project_cross",), ("flip",), ("left_start",), ("own",),
        ("pump", 0), ("pump", 1), ("hear", 1), ("tell", 2), ("left_second",), ("pump", 2), ("left_end",),
        ("mapped",), ("mapped_send",), ("z_first",), ("pump", 3), ("mapped_relay",), ("pump", 4), ("hear", 2),
        ("mapped_end",), ("z_send",), ("pump", 5), ("z_scatter",), ("factor",), ("pump", 6), ("merge", 0),
        ("merge", 1), ("merge", 2), ("pump", 7), ("z_over_y",), ("merge", 3), ("merge", 4), ("merge", 5),
        ("pump", 8), ("z_back",), ("pump", 9), ("merge", 6), ("merge", 7), ("pump", 10), ("z_cross",),
        ("merge", 8), ("z_end",), ("pump", 11), ("finish",), ("merge", 9), ("pump", 12), ("merge", 10),
        ("opposite", 11), ("merge", 11), ("opposite", 12), ("merge", 12), ("leave",),
    ]


def update_kernel(merged, p3, right, out, right_out, stage, r3_v, sems, right_sem):
    d = merged.shape[1]
    width = stage.shape[2]
    steps = d // width
    right_copy = pltpu.make_async_copy(right, right_out, right_sem)
    right_copy.start()

    def block(i):
        return pl.ds(pl.multiple_of(i * width, 128), width)

    def copy(i):
        return pltpu.make_async_copy(stage.at[i], out.at[:, block(i)], sems.at[i])

    for i in range(steps):
        r_high, r_low = split2(right[:, block(i)])
        r3_v[...] = jnp.concatenate([r_high, r_low, r_high, jnp.zeros((RANK, width), BF16)], axis=0)
        stage[i] = (merged[:, block(i)] - dot(p3[...], r3_v[...])).astype(BF16)
        copy(i).start()
    for i in range(steps):
        copy(i).wait()
    right_copy.wait()


def body(nx, nz, activations, out_grads, feedback, right_basis):
    tokens, feat = activations.shape
    tok, d = out_grads.shape
    half = d // 2
    piece = (RANK // nx, half // nz)
    any_spec = pl.BlockSpec(memory_space=pl.ANY)
    vmem_spec = pl.BlockSpec(memory_space=pltpu.VMEM)
    dma = pltpu.SemaphoreType.DMA
    merged, p3, right = pl.pallas_call(
        functools.partial(chain_kernel, nx, nz, chain_plan()),
        out_shape=(
            pltpu.VMEM((feat, d), F32),
            pltpu.VMEM((feat, 128), BF16),
            pltpu.VMEM((RANK, d), F32),
        ),
        in_specs=[any_spec] * 4,
        out_specs=(vmem_spec,) * 3,
        scratch_shapes=[
            pltpu.VMEM((tokens, feat), BF16),
            pltpu.VMEM((feat, tokens), BF16),
            pltpu.VMEM((tokens, d), BF16),
            pltpu.VMEM((feat, d), BF16),
            pltpu.VMEM((RANK, d), F32),
            pltpu.VMEM((2 * RANK, d), BF16),
            pltpu.VMEM((2, NY, RANK, tok), F32),
            pltpu.VMEM((feat, 2 * RANK), F32),
            pltpu.VMEM((nx, RANK // 2, feat), BF16),
            pltpu.VMEM((nz, RANK // 2, feat), BF16),
            pltpu.VMEM((nz, RANK // 2, feat), BF16),
            pltpu.VMEM((nx, RANK // 2, feat), BF16),
            pltpu.VMEM((RANK, feat), F32),
            pltpu.VMEM((2 * RANK, feat), BF16),
            pltpu.VMEM((2, NY, RANK + 8, tok), F32),
            pltpu.VMEM((NY, RANK + 8, tok), F32),
            pltpu.VMEM((NY, RANK + 8, tok), F32),
            pltpu.VMEM((RANK, tok), F32),
            pltpu.VMEM((RANK, tok), F32),
            pltpu.VMEM((2 * RANK, tok), BF16),
            pltpu.VMEM((RANK, 128), F32),
            pltpu.VMEM((RANK, d), F32),
            pltpu.VMEM((RANK, half), F32),
            pltpu.VMEM((nx * nz,) + piece, F32),
            pltpu.VMEM((NY,) + piece, F32),
            pltpu.VMEM((RANK, d), F32),
            dma((4,)),
            dma((2 * CHUNKS,)),
            dma((2 * CHUNKS,)),
            dma((3 * CHUNKS,)),
            dma,
            dma((NT,)),
            dma((nx + nz,)),
            dma((nx + nz,)),
            dma,
            dma((NY,)),
            dma,
            dma,
            dma((nx * nz,)),
            dma((NY,)),
            dma((nx * nz,)),
            dma,
            dma((22,)),
            pltpu.SemaphoreType.REGULAR((3,)),
        ],
        compiler_params=pltpu.CompilerParams(
            collective_id=0, has_side_effects=True, vmem_limit_bytes=VMEM_LIMIT
        ),
        name="gather_and_factors",
    )(activations, out_grads, feedback[0], right_basis.T)
    width = min(512, d // 2)
    vmem = functools.partial(pltpu.with_memory_space_constraint, memory_space=pltpu.VMEM)
    new_feedback, new_right = pl.pallas_call(
        update_kernel,
        out_shape=(
            jax.ShapeDtypeStruct((feat, d), BF16),
            jax.ShapeDtypeStruct((RANK, d), F32),
        ),
        in_specs=[vmem_spec] * 3,
        out_specs=(any_spec, any_spec),
        scratch_shapes=[
            pltpu.VMEM((d // width, feat, width), BF16),
            pltpu.VMEM((128, width), BF16),
            dma((d // width,)),
            dma,
        ],
        compiler_params=pltpu.CompilerParams(vmem_limit_bytes=16 << 20),
        name="update",
    )(vmem(merged), vmem(p3), vmem(right))
    return new_feedback[None], new_right.T


VMEM_LIMIT = 40 << 20


def solution(mesh):
    nx = nz = 4
    in_specs = (P("dp", "tensor"), P(("dp", "tensor"), None), P("dp", "tensor", None), P())
    out_specs = (P("dp", "tensor", None), P())
    return jax.shard_map(
        functools.partial(body, nx, nz), mesh=mesh, in_specs=in_specs, out_specs=out_specs, check_vma=False
    )
```

```python
import functools

import jax
import jax.numpy as jnp
from jax import lax
from jax.experimental import pallas as pl
from jax.experimental.pallas import tpu as pltpu
from jax.sharding import PartitionSpec as P

MESH = pl.DeviceIdType.MESH
F32 = jnp.float32
BF16 = jnp.bfloat16
HIGHEST = lax.Precision.HIGHEST
RANK = 32
AHEAD = 5
NY = 4
NT = 8
WIDTHS = (256,) + (512,) * 11 + (256,)
STARTS = tuple(sum(WIDTHS[:k]) for k in range(len(WIDTHS)))
CHUNKS = len(WIDTHS)
ROWS_FIRST = (((1,), (0,)), ((), ()))
ROWS_BOTH = (((1,), (1,)), ((), ()))


def dot(a, b, dims=ROWS_FIRST, precision=None):
    return lax.dot_general(a, b, dims, precision=precision, preferred_element_type=F32)


def split2(x):
    high = x.astype(BF16)
    low = (x - high.astype(F32)).astype(BF16)
    return high, low


def split3(x):
    high, low = split2(x)
    return high, low, (x - high.astype(F32) - low.astype(F32)).astype(BF16)


def inverse_factor(gram):
    row = lax.broadcasted_iota(jnp.int32, (RANK, 128), 0)
    lane = lax.broadcasted_iota(jnp.int32, (RANK, 128), 1)
    work = jnp.where(lane < RANK, gram, jnp.where(lane == row + RANK, 1.0, 0.0))
    for k in range(RANK):
        column = jnp.broadcast_to(work[:, k : k + 1], (RANK, 128))
        pivot = column[k : k + 1, :]
        inv = lax.rsqrt(pivot)
        inv = inv * (1.5 - 0.5 * pivot * inv * inv)
        scaled = work[k : k + 1, :] * inv
        factor = jnp.where(row > k, column * inv, 0.0)
        work = jnp.where(row == k, scaled, work - factor * scaled)
    return work[:, RANK : 2 * RANK]


def chain_kernel(
    nx, nz, plan,
    a_hbm, g_hbm, f_hbm, q_hbm,
    merged, p3, right,
    a_v, at_v, g_v, f_v, q_v, q2_v, gq_s, fq_v,
    la1, lb1, la2, lb2, left_v, left2_v,
    al_send, al_sib, al_s, al_fwd, al_in, al2_v, linv_v,
    z_v, zsib, rs_s, y_s, zf,
    load_sem, dir_r, rel_r, sib_r, own_r, gq_r, l1_r, l2_r, als_r, al_r, ali_r, zs_r, rs_r, y_r, ag_r, zf_r, send_sem, round_sem, ring_sem,
):
    tok, d = g_hbm.shape
    feat = f_hbm.shape[0]
    half = d // 2
    piece_r, piece_c = RANK // nx, half // nz
    zw = min(512, d)
    hw = min(512, half)
    hr = RANK // 2
    dp, t = lax.axis_index("dp"), lax.axis_index("tensor")
    x, z = dp // nz, dp % nz
    y, c = t // 2, t % 2
    yp, ym, y2 = (y + 1) % NY, (y + 3) % NY, (y + 2) % NY
    sib = (dp, y * 2 + 1 - c)
    mine, other = c * half, (1 - c) * half
    my_half = pl.ds(pl.multiple_of(mine, 128), half)
    sib_half = pl.ds(pl.multiple_of(other, 128), half)
    dp_peers = [(((x + i) % nx), ((z + k) % nz)) for i in range(nx) for k in range(nz) if i or k]
    x_peers = [((x + i) % nx) for i in range(1, nx)]
    z_peers = [((z + i) % nz) for i in range(1, nz)]
    outgoing = []

    def at_y(yy):
        return (dp, yy * 2 + c)

    def rows(tt, first=0, count=None):
        return pl.ds(pl.multiple_of(tt * tok + first, 16), tok if count is None else count)

    def cols(j):
        return pl.ds(STARTS[j], WIDTHS[j])

    def remote(src, dst, send, recv, device):
        return pltpu.make_async_remote_copy(
            src_ref=src, dst_ref=dst, send_sem=send, recv_sem=recv, device_id=device, device_id_type=MESH
        )

    def send(src, dst, sem, recv, device):
        remote(src, dst, send_sem.at[sem], recv, device).start()
        outgoing.append(sem)

    def receive(ref, recv):
        remote(ref, ref, send_sem.at[0], recv, sib).wait_recv()

    def piece(xx, zz):
        return (
            pl.ds(pl.multiple_of((xx + NY - y) % nx * piece_r, 8), piece_r),
            pl.ds(pl.multiple_of(mine + zz * piece_c, 128), piece_c),
        )

    def total(slots, n):
        out = slots[0].astype(F32)
        for k in range(1, n):
            out = out + slots[k].astype(F32)
        return out

    loads = [
        pltpu.make_async_copy(g_hbm, g_v.at[rows(t), :], load_sem.at[0]),
        pltpu.make_async_copy(q_hbm, q_v, load_sem.at[1]),
        pltpu.make_async_copy(f_hbm, f_v, load_sem.at[2]),
        pltpu.make_async_copy(a_hbm, a_v, load_sem.at[3]),
    ]

    before = [(x > 0, (dp - nz, t)), (z > 0, (dp - 1, t))]
    after = [(x < nx - 1, (dp + nz, t)), (z < nz - 1, (dp + 1, t))]
    ring = [at_y(yp), at_y(ym)]

    def signal(sem, devices):
        for there, device in devices:

            @pl.when(there)
            def _():
                pl.semaphore_signal(sem, 1, device_id=device, device_id_type=MESH)

    def count(devices):
        return sum(there.astype(jnp.int32) for there, _ in devices)

    def enter():
        loads[0].start()
        loads[1].start()
        barrier = pltpu.get_barrier_semaphore()
        for device in ring + [sib]:
            pl.semaphore_signal(barrier, 1, device_id=device, device_id_type=MESH)
        signal(barrier, after)
        loads[0].wait()
        loads[2].start()
        loads[3].start()
        loads[1].wait()
        q2_v[...] = jnp.concatenate(split2(q_v[...]), axis=0)
        pl.semaphore_wait(barrier, 3 + count(before))
        for device in ring:
            pl.semaphore_signal(ring_sem, 1, device_id=device, device_id_type=MESH)

    def hear_ring():
        pl.semaphore_wait(ring_sem, 2)

    def tell(k):
        signal(round_sem.at[k], before + after if k else before)

    def hear(k):
        told = count(before + after if k else after)

        @pl.when(told > 0)
        def _():
            pl.semaphore_wait(round_sem.at[k], told)

    def wait_load(k):
        loads[k].wait()


    def own():
        send(g_v.at[rows(t), :], g_v.at[rows(t), :], 0, own_r, sib)

    def direct(j):
        block = g_v.at[rows(t), cols(j)]
        send(block, block, 1, dir_r.at[2 * j], at_y(yp))
        send(block, block, 2, dir_r.at[2 * j + 1], at_y(ym))

    def to_sib(tt, j, k):
        block = g_v.at[rows(tt), cols(j)]
        send(block, block, 3 + k, sib_r.at[3 * j + k], sib)

    def relay(j):
        receive(g_v.at[rows(ym * 2 + c), cols(j)], dir_r.at[2 * j])
        block = g_v.at[rows(ym * 2 + c, 0, tok // 2), cols(j)]
        send(block, block, 6, rel_r.at[2 * j], at_y(yp))
        receive(g_v.at[rows(yp * 2 + c), cols(j)], dir_r.at[2 * j + 1])
        block = g_v.at[rows(yp * 2 + c, tok // 2, tok // 2), cols(j)]
        send(block, block, 7, rel_r.at[2 * j + 1], at_y(ym))

    def cross(j):
        to_sib(ym * 2 + c, j, 0)
        to_sib(yp * 2 + c, j, 1)

    def opposite(j):
        receive(g_v.at[rows(y2 * 2 + c, 0, tok // 2), cols(j)], rel_r.at[2 * j])
        receive(g_v.at[rows(y2 * 2 + c, tok // 2, tok // 2), cols(j)], rel_r.at[2 * j + 1])
        to_sib(y2 * 2 + c, j, 2)

    def pump(j, ahead=True):
        relay(j)
        if ahead and j + AHEAD < CHUNKS:
            direct(j + AHEAD)
        cross(j)

    def absorb(j, part=None):
        if j == 0 and part != 1:
            receive(g_v.at[rows(sib[1]), :], own_r)
        for k, yy in enumerate((ym, yp, y2)):
            if part is None or (part == 1) == (k == 2):
                receive(g_v.at[rows(yy * 2 + 1 - c), cols(j)], sib_r.at[3 * j + k])

    def merge(j, part=None):
        absorb(j, part)
        width = min(256, WIDTHS[j])

        def chips(at, *ys):
            out = None
            for yy in ys:
                pair = pl.ds(pl.multiple_of(yy * 2 * tok, 2 * tok), 2 * tok)
                term = dot(at_v[:, pair], g_v[pair, at])
                out = term if out is None else out + term
            return out

        def step(i, carry):
            at = pl.ds(pl.multiple_of(STARTS[j] + i * width, 128), width)
            if part is None:
                merged[:, at] = dot(at_v[...], g_v[:, at]) + f_v[:, at].astype(F32)
            elif part == 0:
                merged[:, at] = chips(at, y, yp, ym) + f_v[:, at].astype(F32)
            else:
                merged[:, at] += chips(at, y2)
            return carry

        lax.fori_loop(0, WIDTHS[j] // width, step, 0)


    y_peers = (yp, y2, ym)

    def project():
        gq2 = dot(q2_v[...], g_v[rows(t), :], ROWS_BOTH)
        gq_s[c, y] = gq2[:RANK] + gq2[RANK:]

    def project_send():
        for yy in y_peers:
            send(gq_s.at[c, y], gq_s.at[c, y], 8, gq_r.at[y], at_y(yy))
        send(gq_s.at[c, y], gq_s.at[c, y], 19, gq_r.at[NY + y], sib)

    def project_cross():
        for yy in y_peers:
            receive(gq_s.at[c, yy], gq_r.at[yy])
            send(gq_s.at[c, yy], gq_s.at[c, yy], 19, gq_r.at[NY + yy], sib)

    def carried():
        wait_load(2)
        depth = d // 3
        for k in range(d // depth):
            at = pl.ds(k * depth, depth)
            part = dot(f_v[:, at], q2_v[:, at], ROWS_BOTH)
            if k == 0:
                fq_v[...] = part
            else:
                fq_v[...] += part

    def flip():
        wait_load(3)
        for k in range(NT):
            at_v[:, k * tok : (k + 1) * tok] = jnp.transpose(a_v[k * tok : (k + 1) * tok, :])

    def left_start():
        for yy in range(NY):
            receive(gq_s.at[1 - c, yy], gq_r.at[NY + yy])
        gq = jnp.concatenate([gq_s[k % 2, k // 2] for k in range(NT)], axis=1)
        part = dot(jnp.concatenate(split2(gq), axis=0), a_v[...])
        fq = fq_v[...]
        left_part = part[:RANK] + part[RANK:] + jnp.transpose(fq[:, :RANK] + fq[:, RANK:])
        la1[x] = left_part[:hr].astype(BF16)
        lb1[z] = left_part[hr:].astype(BF16)
        left_send(la1, lb1, l1_r, 9)

    def left_send(slots_x, slots_z, sems, at):
        for xx in x_peers:
            send(slots_x.at[x], slots_x.at[x], at, sems.at[x], (xx * nz + z, t))
        for zz in z_peers:
            send(slots_z.at[z], slots_z.at[z], at + 1, sems.at[nx + z], (x * nz + zz, t))

    def left_receive(slots_x, slots_z, sems):
        for xx in x_peers:
            receive(slots_x.at[xx], sems.at[xx])
        for zz in z_peers:
            receive(slots_z.at[zz], sems.at[nx + zz])

    def left_second():
        left_receive(la1, lb1, l1_r)
        la2[z] = total(la1, nx).astype(BF16)
        lb2[x] = total(lb1, nz).astype(BF16)
        left_send(lb2, la2, l2_r, 11)

    def left_end():
        left_receive(lb2, la2, l2_r)
        left_v[:hr] = total(la2, nz)
        left_v[hr:] = total(lb2, nx)
        left2_v[...] = jnp.concatenate(split2(left_v[...]), axis=0)

    def mapped():
        left = left_v[...]
        al = dot(left2_v[...], at_v[...])
        al = al[:RANK] + al[RANK:]
        gram = dot(left, left, ROWS_BOTH, HIGHEST)
        gram = jnp.concatenate([gram[8 * k : 8 * k + 8] for k in range(RANK // 8)], axis=1)
        for k in range(NT):
            al_send[k % 2, k // 2, :RANK] = al[:, k * tok : (k + 1) * tok]
            al_send[k % 2, k // 2, RANK:] = gram
        send(al_send.at[1 - c], al_sib, 20, als_r, sib)

    def mapped_send():
        receive(al_sib, als_r)
        al_send[c] += al_sib[...]
        for yy in y_peers:
            send(al_send.at[c, yy], al_s.at[y], 13, al_r.at[y], (((x + 1) % nx) * nz + z, yy * 2 + c))

    def mapped_relay():
        for yy in y_peers:
            receive(al_s.at[yy], al_r.at[yy])
        al_s[y] = al_send[c, y]
        fwd = al_s[yp, :RANK] + al_s[y2, :RANK] + al_s[ym, :RANK]
        al_fwd[...] = fwd
        send(al_fwd, al_in, 21, ali_r, (((x + nx - 1) % nx) * nz + z, t))
        gram = total(al_s, NY)[RANK:]
        gram = jnp.concatenate([gram[:, RANK * k : RANK * (k + 1)] for k in range(RANK // 8)], axis=0)
        linv_v[...] = jnp.concatenate([gram, jnp.zeros((RANK, 128 - RANK), F32)], axis=1)

    def z_first():
        def step(i, carry):
            at = pl.ds(pl.multiple_of(i * zw, 128), zw)
            r = dot(left2_v[...], f_v[:, at])
            z_v[:, at] = r[:RANK] + r[RANK:]
            return carry

        lax.fori_loop(0, d // zw, step, 0)

    def mapped_end():
        receive(al_in, ali_r)
        al2_v[...] = jnp.concatenate(split2(al_send[c, y, :RANK] + al_in[...]), axis=0)

    def z_second(base):
        def step(i, carry):
            at = pl.ds(pl.multiple_of(base + i * hw, 128), hw)
            r = dot(al2_v[...], g_v[rows(t), at])
            z_v[:, at] += r[:RANK] + r[RANK:]
            return carry

        lax.fori_loop(0, half // hw, step, 0)

    def z_send():
        z_second(other)
        send(z_v.at[:, sib_half], zsib, 14, zs_r, sib)
        z_second(mine)

    def z_scatter():
        receive(zsib, zs_r)
        z_v[:, my_half] += zsib[...]
        for xx, zz in dp_peers:
            send(z_v.at[piece(xx, zz)], rs_s.at[dp], 15, rs_r.at[dp], (xx * nz + zz, t))
        rs_s[dp] = z_v[piece(x, z)]

    def factor():
        linv = inverse_factor(linv_v[...])
        linv_v[:, :RANK] = linv
        p_high, p_low = split2(dot(linv, left_v[...], precision=HIGHEST))
        p_rows = jnp.concatenate([p_high, p_high, p_low, jnp.zeros((RANK, feat), BF16)], axis=0)
        p3[...] = jnp.transpose(p_rows.astype(F32)).astype(BF16)

    def z_over_y():
        for xx, zz in dp_peers:
            receive(rs_s.at[xx * nz + zz], rs_r.at[xx * nz + zz])
        y_s[y] = total(rs_s, nx * nz)
        for yy in (yp, y2, ym):
            send(y_s.at[y], y_s.at[y], 16, y_r.at[y], (((x + NY - y + yy) % nx) * nz + z, yy * 2 + c))

    def z_back():
        for yy in (yp, y2, ym):
            receive(y_s.at[yy], y_r.at[yy])
        ours = piece(x, z)
        zf[ours] = total(y_s, NY)
        for xx, zz in dp_peers:
            send(zf.at[ours], zf.at[ours], 17, ag_r.at[dp], (xx * nz + zz, t))
        send(zf.at[ours], zf.at[ours], 18, zf_r, sib)

    def z_cross():
        for xx, zz in dp_peers:
            theirs = piece(xx, zz)
            receive(zf.at[theirs], ag_r.at[xx * nz + zz])
            send(zf.at[theirs], zf.at[theirs], 18, zf_r, sib)

    def z_end():
        receive(zf.at[:, sib_half], zf_r)

    def finish():
        l1, l2, l3 = split3(linv_v[:, :RANK])
        lhs = jnp.concatenate([l1, l1, l2, l1, l2, l3], axis=1)

        fw = d // 4

        def step(i, carry):
            at = pl.ds(pl.multiple_of(i * fw, 128), fw)
            z1, z2, z3 = split3(zf[:, at])
            rhs = jnp.concatenate([z1, z2, z1, z3, z2, z1], axis=0)
            right[:, at] = dot(lhs, rhs) * (1.0 / (nx * nz))
            return carry

        lax.fori_loop(0, d // fw, step, 0)

    def leave():
        gather = [g_v.at[rows(t), :]] * 6 + [g_v.at[rows(t, 0, tok // 2), :]] * 2
        pieces = gather + [gq_s.at[0, pl.ds(0, NY - 1)]]
        for slots in (la1, lb1, lb2, la2):
            pieces.append(slots.at[pl.ds(0, slots.shape[0] - 1)])
        pieces += [al_s.at[pl.ds(0, NY - 1)], zsib, rs_s.at[pl.ds(0, nx * nz - 1)]]
        pieces += [y_s.at[pl.ds(0, NY - 1)], rs_s.at[pl.ds(0, nx * nz - 1)], zsib]
        pieces += [gq_s.at[0], al_sib, al_in]
        for sem, ref in enumerate(pieces):
            if sem in outgoing:
                remote(ref, ref, send_sem.at[sem], own_r, sib).wait_send()

    steps = dict(tell=tell, hear=hear, hear_ring=hear_ring, project_send=project_send, project_cross=project_cross,
        enter=enter, wait_load=wait_load, absorb=absorb, own=own, direct=direct, relay=relay, cross=cross, opposite=opposite, pump=pump, merge=merge,
        project=project, carried=carried, flip=flip, left_start=left_start, left_second=left_second,
        left_end=left_end, mapped=mapped, mapped_send=mapped_send, mapped_relay=mapped_relay, z_first=z_first, mapped_end=mapped_end,
        z_send=z_send, z_scatter=z_scatter, factor=factor, z_over_y=z_over_y, z_back=z_back, z_cross=z_cross,
        z_end=z_end, finish=finish, leave=leave,
    )
    for name, *args in plan:
        steps[name](*args)


def chain_plan():
    return [
        ("enter",), ("direct", 0), ("project",), ("hear_ring",), ("project_send",), ("tell", 0), ("direct", 1),
        ("direct", 2), ("direct", 3), ("direct", 4), ("hear", 0), ("tell", 1), ("carried",), ("hear", 1),
        ("tell", 2), ("project_cross",), ("flip",), ("hear", 2), ("tell", 3), ("left_start",), ("own",),
        ("pump", 0), ("hear", 3), ("tell", 4), ("pump", 1), ("left_second",), ("hear", 4), ("tell", 5),
        ("pump", 2), ("pump", 3), ("pump", 4), ("left_end",), ("mapped",), ("mapped_send",), ("z_first",),
        ("opposite", 0), ("mapped_relay",), ("pump", 5), ("opposite", 1), ("hear", 5), ("mapped_end",),
        ("z_send",), ("pump", 6), ("opposite", 2), ("z_scatter",), ("factor",), ("pump", 7), ("opposite", 3),
        ("merge", 0), ("merge", 1), ("merge", 2), ("pump", 8), ("opposite", 4), ("z_over_y",), ("pump", 9),
        ("opposite", 5), ("merge", 3), ("merge", 4), ("z_back",), ("pump", 10), ("opposite", 6), ("merge", 5),
        ("pump", 11), ("opposite", 7), ("merge", 6), ("merge", 7), ("merge", 8, 0), ("merge", 9, 0), ("pump", 12),
        ("z_cross",), ("opposite", 8), ("opposite", 9), ("merge", 8, 1), ("opposite", 10), ("merge", 9, 1),
        ("z_end",), ("finish",), ("merge", 10), ("opposite", 11), ("merge", 11, 0), ("merge", 12, 0),
        ("opposite", 12), ("merge", 11, 1), ("merge", 12, 1), ("leave",),
    ]


def update_kernel(merged, p3, right, out, right_out, stage, r3_v, sems, right_sem):
    d = merged.shape[1]
    width = stage.shape[2]
    steps = d // width
    right_copy = pltpu.make_async_copy(right, right_out, right_sem)
    right_copy.start()

    def block(i):
        return pl.ds(pl.multiple_of(i * width, 128), width)

    def copy(i):
        return pltpu.make_async_copy(stage.at[i], out.at[:, block(i)], sems.at[i])

    for i in range(steps):
        r_high, r_low = split2(right[:, block(i)])
        r3_v[...] = jnp.concatenate([r_high, r_low, r_high, jnp.zeros((RANK, width), BF16)], axis=0)
        stage[i] = (merged[:, block(i)] - dot(p3[...], r3_v[...])).astype(BF16)
        copy(i).start()
    for i in range(steps):
        copy(i).wait()
    right_copy.wait()


def body(nx, nz, activations, out_grads, feedback, right_basis):
    tokens, feat = activations.shape
    tok, d = out_grads.shape
    half = d // 2
    piece = (RANK // nx, half // nz)
    any_spec = pl.BlockSpec(memory_space=pl.ANY)
    vmem_spec = pl.BlockSpec(memory_space=pltpu.VMEM)
    dma = pltpu.SemaphoreType.DMA
    merged, p3, right = pl.pallas_call(
        functools.partial(chain_kernel, nx, nz, chain_plan()),
        out_shape=(
            pltpu.VMEM((feat, d), F32),
            pltpu.VMEM((feat, 128), BF16),
            pltpu.VMEM((RANK, d), F32),
        ),
        in_specs=[any_spec] * 4,
        out_specs=(vmem_spec,) * 3,
        scratch_shapes=[
            pltpu.VMEM((tokens, feat), BF16),
            pltpu.VMEM((feat, tokens), BF16),
            pltpu.VMEM((tokens, d), BF16),
            pltpu.VMEM((feat, d), BF16),
            pltpu.VMEM((RANK, d), F32),
            pltpu.VMEM((2 * RANK, d), BF16),
            pltpu.VMEM((2, NY, RANK, tok), F32),
            pltpu.VMEM((feat, 2 * RANK), F32),
            pltpu.VMEM((nx, RANK // 2, feat), BF16),
            pltpu.VMEM((nz, RANK // 2, feat), BF16),
            pltpu.VMEM((nz, RANK // 2, feat), BF16),
            pltpu.VMEM((nx, RANK // 2, feat), BF16),
            pltpu.VMEM((RANK, feat), F32),
            pltpu.VMEM((2 * RANK, feat), BF16),
            pltpu.VMEM((2, NY, RANK + 8, tok), F32),
            pltpu.VMEM((NY, RANK + 8, tok), F32),
            pltpu.VMEM((NY, RANK + 8, tok), F32),
            pltpu.VMEM((RANK, tok), F32),
            pltpu.VMEM((RANK, tok), F32),
            pltpu.VMEM((2 * RANK, tok), BF16),
            pltpu.VMEM((RANK, 128), F32),
            pltpu.VMEM((RANK, d), F32),
            pltpu.VMEM((RANK, half), F32),
            pltpu.VMEM((nx * nz,) + piece, F32),
            pltpu.VMEM((NY,) + piece, F32),
            pltpu.VMEM((RANK, d), F32),
            dma((4,)),
            dma((2 * CHUNKS,)),
            dma((2 * CHUNKS,)),
            dma((3 * CHUNKS,)),
            dma,
            dma((NT,)),
            dma((nx + nz,)),
            dma((nx + nz,)),
            dma,
            dma((NY,)),
            dma,
            dma,
            dma((nx * nz,)),
            dma((NY,)),
            dma((nx * nz,)),
            dma,
            dma((22,)),
            pltpu.SemaphoreType.REGULAR((6,)),
            pltpu.SemaphoreType.REGULAR,
        ],
        compiler_params=pltpu.CompilerParams(
            collective_id=0, has_side_effects=True, vmem_limit_bytes=VMEM_LIMIT
        ),
        name="gather_and_factors",
    )(activations, out_grads, feedback[0], right_basis.T)
    width = min(512, d // 2)
    vmem = functools.partial(pltpu.with_memory_space_constraint, memory_space=pltpu.VMEM)
    new_feedback, new_right = pl.pallas_call(
        update_kernel,
        out_shape=(
            jax.ShapeDtypeStruct((feat, d), BF16),
            jax.ShapeDtypeStruct((RANK, d), F32),
        ),
        in_specs=[vmem_spec] * 3,
        out_specs=(any_spec, any_spec),
        scratch_shapes=[
            pltpu.VMEM((d // width, feat, width), BF16),
            pltpu.VMEM((128, width), BF16),
            dma((d // width,)),
            dma,
        ],
        compiler_params=pltpu.CompilerParams(vmem_limit_bytes=16 << 20),
        name="update",
    )(vmem(merged), vmem(p3), vmem(right))
    return new_feedback[None], new_right.T


VMEM_LIMIT = 40 << 20


def solution(mesh):
    nx = nz = 4
    in_specs = (P("dp", "tensor"), P(("dp", "tensor"), None), P("dp", "tensor", None), P())
    out_specs = (P("dp", "tensor", None), P())
    return jax.shard_map(
        functools.partial(body, nx, nz), mesh=mesh, in_specs=in_specs, out_specs=out_specs, check_vma=False
    )
```

```python
import functools

import jax
import jax.numpy as jnp
from jax import lax
from jax.experimental import pallas as pl
from jax.experimental.pallas import tpu as pltpu
from jax.sharding import PartitionSpec as P

MESH = pl.DeviceIdType.MESH
F32 = jnp.float32
BF16 = jnp.bfloat16
HIGHEST = lax.Precision.HIGHEST
RANK = 32
AHEAD = 4
NY = 4
NT = 8
WIDTHS = (512,) * 11 + (256, 256)
STARTS = tuple(sum(WIDTHS[:k]) for k in range(len(WIDTHS)))
CHUNKS = len(WIDTHS)
ROWS_FIRST = (((1,), (0,)), ((), ()))
ROWS_BOTH = (((1,), (1,)), ((), ()))


def dot(a, b, dims=ROWS_FIRST, precision=None):
    return lax.dot_general(a, b, dims, precision=precision, preferred_element_type=F32)


def split2(x):
    high = x.astype(BF16)
    low = (x - high.astype(F32)).astype(BF16)
    return high, low


def split3(x):
    high, low = split2(x)
    return high, low, (x - high.astype(F32) - low.astype(F32)).astype(BF16)


def inverse_factor(gram):
    row = lax.broadcasted_iota(jnp.int32, (RANK, 128), 0)
    lane = lax.broadcasted_iota(jnp.int32, (RANK, 128), 1)
    work = jnp.where(lane < RANK, gram, jnp.where(lane == row + RANK, 1.0, 0.0))
    for k in range(RANK):
        column = jnp.broadcast_to(work[:, k : k + 1], (RANK, 128))
        pivot = column[k : k + 1, :]
        inv = lax.rsqrt(pivot)
        inv = inv * (1.5 - 0.5 * pivot * inv * inv)
        scaled = work[k : k + 1, :] * inv
        factor = jnp.where(row > k, column * inv, 0.0)
        work = jnp.where(row == k, scaled, work - factor * scaled)
    return work[:, RANK : 2 * RANK]


def chain_kernel(
    nx, nz, plan,
    a_hbm, g_hbm, f_hbm, q_hbm,
    merged, p3, right,
    a_v, at_v, g_v, f_v, q_v, q2_v, gq_s, fq_v,
    la1, lb1, la2, lb2, left_v, left2_v,
    al_send, al_sib, al_s, al_fwd, al_in, al2_v, linv_v,
    z_v, zsib, rs_s, y_s, zf,
    load_sem, dir_r, rel_r, sib_r, own_r, gq_r, l1_r, l2_r, als_r, al_r, ali_r, zs_r, rs_r, y_r, ag_r, zf_r, send_sem, round_sem, ring_sem,
):
    tok, d = g_hbm.shape
    feat = f_hbm.shape[0]
    half = d // 2
    piece_r, piece_c = RANK // nx, half // nz
    zw = min(512, d)
    hw = min(512, half)
    hr = RANK // 2
    dp, t = lax.axis_index("dp"), lax.axis_index("tensor")
    x, z = dp // nz, dp % nz
    y, c = t // 2, t % 2
    yp, ym, y2 = (y + 1) % NY, (y + 3) % NY, (y + 2) % NY
    sib = (dp, y * 2 + 1 - c)
    mine, other = c * half, (1 - c) * half
    my_half = pl.ds(pl.multiple_of(mine, 128), half)
    sib_half = pl.ds(pl.multiple_of(other, 128), half)
    dp_peers = [(((x + i) % nx), ((z + k) % nz)) for i in range(nx) for k in range(nz) if i or k]
    x_peers = [((x + i) % nx) for i in range(1, nx)]
    z_peers = [((z + i) % nz) for i in range(1, nz)]
    outgoing = []

    def at_y(yy):
        return (dp, yy * 2 + c)

    def rows(tt, first=0, count=None):
        return pl.ds(pl.multiple_of(tt * tok + first, 16), tok if count is None else count)

    def cols(j):
        return pl.ds(STARTS[j], WIDTHS[j])

    def remote(src, dst, send, recv, device):
        return pltpu.make_async_remote_copy(
            src_ref=src, dst_ref=dst, send_sem=send, recv_sem=recv, device_id=device, device_id_type=MESH
        )

    def send(src, dst, sem, recv, device):
        remote(src, dst, send_sem.at[sem], recv, device).start()
        outgoing.append(sem)

    def receive(ref, recv):
        remote(ref, ref, send_sem.at[0], recv, sib).wait_recv()

    def piece(xx, zz):
        return (
            pl.ds(pl.multiple_of((xx + NY - y) % nx * piece_r, 8), piece_r),
            pl.ds(pl.multiple_of(mine + zz * piece_c, 128), piece_c),
        )

    def total(slots, n):
        out = slots[0].astype(F32)
        for k in range(1, n):
            out = out + slots[k].astype(F32)
        return out

    loads = [
        pltpu.make_async_copy(g_hbm, g_v.at[rows(t), :], load_sem.at[0]),
        pltpu.make_async_copy(q_hbm, q_v, load_sem.at[1]),
        pltpu.make_async_copy(f_hbm, f_v, load_sem.at[2]),
        pltpu.make_async_copy(a_hbm, a_v, load_sem.at[3]),
    ]

    before = [(x > 0, (dp - nz, t)), (z > 0, (dp - 1, t))]
    after = [(x < nx - 1, (dp + nz, t)), (z < nz - 1, (dp + 1, t))]
    ring = [at_y(yp), at_y(ym)]

    def signal(sem, devices):
        for there, device in devices:

            @pl.when(there)
            def _():
                pl.semaphore_signal(sem, 1, device_id=device, device_id_type=MESH)

    def count(devices):
        return sum(there.astype(jnp.int32) for there, _ in devices)

    def enter():
        loads[0].start()
        loads[1].start()
        barrier = pltpu.get_barrier_semaphore()
        for device in ring + [sib]:
            pl.semaphore_signal(barrier, 1, device_id=device, device_id_type=MESH)
        signal(barrier, after)
        loads[0].wait()
        loads[2].start()
        loads[3].start()
        pl.semaphore_wait(barrier, 3 + count(before))
        for device in ring:
            pl.semaphore_signal(ring_sem, 1, device_id=device, device_id_type=MESH)

    def hear_ring():
        pl.semaphore_wait(ring_sem, 2)

    def tell(k):
        signal(round_sem.at[k], before + after if k else before)

    def hear(k):
        told = count(before + after if k else after)

        @pl.when(told > 0)
        def _():
            pl.semaphore_wait(round_sem.at[k], told)

    def wait_load(k):
        loads[k].wait()


    def own():
        send(g_v.at[rows(t), :], g_v.at[rows(t), :], 0, own_r, sib)

    def direct(j):
        block = g_v.at[rows(t), cols(j)]
        send(block, block, 1, dir_r.at[2 * j], at_y(yp))
        send(block, block, 2, dir_r.at[2 * j + 1], at_y(ym))

    def to_sib(tt, j, k):
        block = g_v.at[rows(tt), cols(j)]
        send(block, block, 3 + k, sib_r.at[3 * j + k], sib)

    def relay(j):
        receive(g_v.at[rows(ym * 2 + c), cols(j)], dir_r.at[2 * j])
        block = g_v.at[rows(ym * 2 + c, 0, tok // 2), cols(j)]
        send(block, block, 6, rel_r.at[2 * j], at_y(yp))
        receive(g_v.at[rows(yp * 2 + c), cols(j)], dir_r.at[2 * j + 1])
        block = g_v.at[rows(yp * 2 + c, tok // 2, tok // 2), cols(j)]
        send(block, block, 7, rel_r.at[2 * j + 1], at_y(ym))

    def cross(j):
        to_sib(ym * 2 + c, j, 0)
        to_sib(yp * 2 + c, j, 1)

    def opposite(j):
        receive(g_v.at[rows(y2 * 2 + c, 0, tok // 2), cols(j)], rel_r.at[2 * j])
        receive(g_v.at[rows(y2 * 2 + c, tok // 2, tok // 2), cols(j)], rel_r.at[2 * j + 1])
        to_sib(y2 * 2 + c, j, 2)

    def pump(j, ahead=True):
        relay(j)
        if ahead and j + AHEAD < CHUNKS:
            direct(j + AHEAD)
        cross(j)

    def absorb(j, part=None):
        if j == 0 and part != 1:
            receive(g_v.at[rows(sib[1]), :], own_r)
        for k, yy in enumerate((ym, yp, y2)):
            if part is None or (part == 1) == (k == 2):
                receive(g_v.at[rows(yy * 2 + 1 - c), cols(j)], sib_r.at[3 * j + k])

    def merge(j, part=None):
        absorb(j, part)
        width = min(256, WIDTHS[j])

        def chips(at, *ys):
            out = None
            for yy in ys:
                pair = pl.ds(pl.multiple_of(yy * 2 * tok, 2 * tok), 2 * tok)
                term = dot(at_v[:, pair], g_v[pair, at])
                out = term if out is None else out + term
            return out

        def step(i, carry):
            at = pl.ds(pl.multiple_of(STARTS[j] + i * width, 128), width)
            if part is None:
                merged[:, at] = dot(at_v[...], g_v[:, at]) + f_v[:, at].astype(F32)
            elif part == 0:
                merged[:, at] = chips(at, y, yp, ym) + f_v[:, at].astype(F32)
            else:
                merged[:, at] += chips(at, y2)
            return carry

        lax.fori_loop(0, WIDTHS[j] // width, step, 0)


    y_peers = (yp, y2, ym)

    def project():
        loads[1].wait()
        q2_v[...] = jnp.concatenate(split2(q_v[...]), axis=0)
        gq2 = dot(q2_v[...], g_v[rows(t), :], ROWS_BOTH)
        gq_s[c, y] = gq2[:RANK] + gq2[RANK:]

    def project_send():
        for yy in y_peers:
            send(gq_s.at[c, y], gq_s.at[c, y], 8, gq_r.at[y], at_y(yy))
        send(gq_s.at[c, y], gq_s.at[c, y], 19, gq_r.at[NY + y], sib)

    def project_cross():
        for yy in y_peers:
            receive(gq_s.at[c, yy], gq_r.at[yy])
            send(gq_s.at[c, yy], gq_s.at[c, yy], 19, gq_r.at[NY + yy], sib)

    def carried():
        wait_load(2)
        depth = d // 3
        for k in range(d // depth):
            at = pl.ds(k * depth, depth)
            part = dot(f_v[:, at], q2_v[:, at], ROWS_BOTH)
            if k == 0:
                fq_v[...] = part
            else:
                fq_v[...] += part

    def flip():
        wait_load(3)
        for k in range(NT):
            at_v[:, k * tok : (k + 1) * tok] = jnp.transpose(a_v[k * tok : (k + 1) * tok, :])

    def left_start():
        for yy in range(NY):
            receive(gq_s.at[1 - c, yy], gq_r.at[NY + yy])
        gq = jnp.concatenate([gq_s[k % 2, k // 2] for k in range(NT)], axis=1)
        part = dot(jnp.concatenate(split2(gq), axis=0), a_v[...])
        fq = fq_v[...]
        left_part = part[:RANK] + part[RANK:] + jnp.transpose(fq[:, :RANK] + fq[:, RANK:])
        la1[x] = left_part[:hr].astype(BF16)
        lb1[z] = left_part[hr:].astype(BF16)
        left_send(la1, lb1, l1_r, 9)

    def left_send(slots_x, slots_z, sems, at):
        for xx in x_peers:
            send(slots_x.at[x], slots_x.at[x], at, sems.at[x], (xx * nz + z, t))
        for zz in z_peers:
            send(slots_z.at[z], slots_z.at[z], at + 1, sems.at[nx + z], (x * nz + zz, t))

    def left_receive(slots_x, slots_z, sems):
        for xx in x_peers:
            receive(slots_x.at[xx], sems.at[xx])
        for zz in z_peers:
            receive(slots_z.at[zz], sems.at[nx + zz])

    def left_second():
        left_receive(la1, lb1, l1_r)
        la2[z] = total(la1, nx).astype(BF16)
        lb2[x] = total(lb1, nz).astype(BF16)
        left_send(lb2, la2, l2_r, 11)

    def left_end():
        left_receive(lb2, la2, l2_r)
        left_v[:hr] = total(la2, nz)
        left_v[hr:] = total(lb2, nx)
        left2_v[...] = jnp.concatenate(split2(left_v[...]), axis=0)

    def mapped():
        left = left_v[...]
        al = dot(left2_v[...], at_v[...])
        al = al[:RANK] + al[RANK:]
        gram = dot(left, left, ROWS_BOTH, HIGHEST)
        gram = jnp.concatenate([gram[8 * k : 8 * k + 8] for k in range(RANK // 8)], axis=1)
        for k in range(NT):
            al_send[k % 2, k // 2, :RANK] = al[:, k * tok : (k + 1) * tok]
            al_send[k % 2, k // 2, RANK:] = gram
        send(al_send.at[1 - c], al_sib, 20, als_r, sib)

    def mapped_send():
        receive(al_sib, als_r)
        al_send[c] += al_sib[...]
        for yy in y_peers:
            send(al_send.at[c, yy], al_s.at[y], 13, al_r.at[y], (((x + 1) % nx) * nz + z, yy * 2 + c))

    def mapped_relay():
        for yy in y_peers:
            receive(al_s.at[yy], al_r.at[yy])
        al_s[y] = al_send[c, y]
        fwd = al_s[yp, :RANK] + al_s[y2, :RANK] + al_s[ym, :RANK]
        al_fwd[...] = fwd
        send(al_fwd, al_in, 21, ali_r, (((x + nx - 1) % nx) * nz + z, t))
        gram = total(al_s, NY)[RANK:]
        gram = jnp.concatenate([gram[:, RANK * k : RANK * (k + 1)] for k in range(RANK // 8)], axis=0)
        linv_v[...] = jnp.concatenate([gram, jnp.zeros((RANK, 128 - RANK), F32)], axis=1)

    def z_first():
        def step(i, carry):
            at = pl.ds(pl.multiple_of(i * zw, 128), zw)
            r = dot(left2_v[...], f_v[:, at])
            z_v[:, at] = r[:RANK] + r[RANK:]
            return carry

        lax.fori_loop(0, d // zw, step, 0)

    def mapped_end():
        receive(al_in, ali_r)
        al2_v[...] = jnp.concatenate(split2(al_send[c, y, :RANK] + al_in[...]), axis=0)

    def z_second(base):
        def step(i, carry):
            at = pl.ds(pl.multiple_of(base + i * hw, 128), hw)
            r = dot(al2_v[...], g_v[rows(t), at])
            z_v[:, at] += r[:RANK] + r[RANK:]
            return carry

        lax.fori_loop(0, half // hw, step, 0)

    def z_send():
        z_second(other)
        send(z_v.at[:, sib_half], zsib, 14, zs_r, sib)
        z_second(mine)

    def z_scatter():
        receive(zsib, zs_r)
        z_v[:, my_half] += zsib[...]
        for xx, zz in dp_peers:
            send(z_v.at[piece(xx, zz)], rs_s.at[dp], 15, rs_r.at[dp], (xx * nz + zz, t))
        rs_s[dp] = z_v[piece(x, z)]

    def factor():
        linv = inverse_factor(linv_v[...])
        linv_v[:, :RANK] = linv
        p_high, p_low = split2(dot(linv, left_v[...], precision=HIGHEST))
        p_rows = jnp.concatenate([p_high, p_high, p_low, jnp.zeros((RANK, feat), BF16)], axis=0)
        p3[...] = jnp.transpose(p_rows.astype(F32)).astype(BF16)

    def z_over_y():
        for xx, zz in dp_peers:
            receive(rs_s.at[xx * nz + zz], rs_r.at[xx * nz + zz])
        y_s[y] = total(rs_s, nx * nz)
        for yy in (yp, y2, ym):
            send(y_s.at[y], y_s.at[y], 16, y_r.at[y], (((x + NY - y + yy) % nx) * nz + z, yy * 2 + c))

    def z_back():
        for yy in (yp, y2, ym):
            receive(y_s.at[yy], y_r.at[yy])
        ours = piece(x, z)
        zf[ours] = total(y_s, NY)
        for xx, zz in dp_peers:
            send(zf.at[ours], zf.at[ours], 17, ag_r.at[dp], (xx * nz + zz, t))
        send(zf.at[ours], zf.at[ours], 18, zf_r, sib)

    def z_cross():
        for xx, zz in dp_peers:
            theirs = piece(xx, zz)
            receive(zf.at[theirs], ag_r.at[xx * nz + zz])
            send(zf.at[theirs], zf.at[theirs], 18, zf_r, sib)

    def z_end():
        receive(zf.at[:, sib_half], zf_r)

    def finish():
        l1, l2, l3 = split3(linv_v[:, :RANK])
        lhs = jnp.concatenate([l1, l1, l2, l1, l2, l3], axis=1)

        fw = d // 4

        def step(i, carry):
            at = pl.ds(pl.multiple_of(i * fw, 128), fw)
            z1, z2, z3 = split3(zf[:, at])
            rhs = jnp.concatenate([z1, z2, z1, z3, z2, z1], axis=0)
            right[:, at] = dot(lhs, rhs) * (1.0 / (nx * nz))
            return carry

        lax.fori_loop(0, d // fw, step, 0)

    def leave():
        gather = [g_v.at[rows(t), :]] * 6 + [g_v.at[rows(t, 0, tok // 2), :]] * 2
        pieces = gather + [gq_s.at[0, pl.ds(0, NY - 1)]]
        for slots in (la1, lb1, lb2, la2):
            pieces.append(slots.at[pl.ds(0, slots.shape[0] - 1)])
        pieces += [al_s.at[pl.ds(0, NY - 1)], zsib, rs_s.at[pl.ds(0, nx * nz - 1)]]
        pieces += [y_s.at[pl.ds(0, NY - 1)], rs_s.at[pl.ds(0, nx * nz - 1)], zsib]
        pieces += [gq_s.at[0], al_sib, al_in]
        for sem, ref in enumerate(pieces):
            if sem in outgoing:
                remote(ref, ref, send_sem.at[sem], own_r, sib).wait_send()

    steps = dict(tell=tell, hear=hear, hear_ring=hear_ring, project_send=project_send, project_cross=project_cross,
        enter=enter, wait_load=wait_load, absorb=absorb, own=own, direct=direct, relay=relay, cross=cross, opposite=opposite, pump=pump, merge=merge,
        project=project, carried=carried, flip=flip, left_start=left_start, left_second=left_second,
        left_end=left_end, mapped=mapped, mapped_send=mapped_send, mapped_relay=mapped_relay, z_first=z_first, mapped_end=mapped_end,
        z_send=z_send, z_scatter=z_scatter, factor=factor, z_over_y=z_over_y, z_back=z_back, z_cross=z_cross,
        z_end=z_end, finish=finish, leave=leave,
    )
    for name, *args in plan:
        steps[name](*args)


def chain_plan():
    return [
        ("enter",), ("direct", 0), ("project",), ("hear_ring",), ("project_send",), ("tell", 0), ("direct", 1),
        ("direct", 2), ("direct", 3), ("hear", 0), ("tell", 1), ("carried",), ("hear", 1), ("tell", 2),
        ("project_cross",), ("flip",), ("hear", 2), ("tell", 3), ("left_start",), ("own",), ("pump", 0),
        ("hear", 3), ("tell", 4), ("pump", 1), ("left_second",), ("hear", 4), ("tell", 5), ("pump", 2),
        ("pump", 3), ("pump", 4), ("left_end",), ("mapped",), ("mapped_send",), ("z_first",), ("opposite", 0),
        ("mapped_relay",), ("pump", 5), ("opposite", 1), ("hear", 5), ("mapped_end",), ("z_send",), ("pump", 6),
        ("opposite", 2), ("z_scatter",), ("factor",), ("pump", 7), ("opposite", 3), ("merge", 0), ("merge", 1),
        ("merge", 2), ("pump", 8), ("opposite", 4), ("z_over_y",), ("pump", 9), ("opposite", 5), ("merge", 3),
        ("merge", 4), ("z_back",), ("pump", 10), ("opposite", 6), ("merge", 5), ("pump", 11), ("opposite", 7),
        ("merge", 6), ("merge", 7), ("pump", 12), ("merge", 8, 0), ("merge", 9, 0), ("z_cross",), ("opposite", 8),
        ("opposite", 9), ("opposite", 10), ("merge", 8, 1), ("merge", 9, 1), ("opposite", 11), ("merge", 10),
        ("z_end",), ("opposite", 12), ("finish",), ("merge", 11), ("merge", 12), ("leave",),
    ]


def update_kernel(merged, p3, right, out, right_out, stage, r3_v, sems, right_sem):
    d = merged.shape[1]
    width = stage.shape[2]
    steps = d // width
    right_copy = pltpu.make_async_copy(right, right_out, right_sem)
    right_copy.start()

    def block(i):
        return pl.ds(pl.multiple_of(i * width, 128), width)

    def copy(i):
        return pltpu.make_async_copy(stage.at[i], out.at[:, block(i)], sems.at[i])

    for i in range(steps):
        r_high, r_low = split2(right[:, block(i)])
        r3_v[...] = jnp.concatenate([r_high, r_low, r_high, jnp.zeros((RANK, width), BF16)], axis=0)
        stage[i] = (merged[:, block(i)] - dot(p3[...], r3_v[...])).astype(BF16)
        copy(i).start()
    for i in range(steps):
        copy(i).wait()
    right_copy.wait()


def body(nx, nz, activations, out_grads, feedback, right_basis):
    tokens, feat = activations.shape
    tok, d = out_grads.shape
    half = d // 2
    piece = (RANK // nx, half // nz)
    any_spec = pl.BlockSpec(memory_space=pl.ANY)
    vmem_spec = pl.BlockSpec(memory_space=pltpu.VMEM)
    dma = pltpu.SemaphoreType.DMA
    merged, p3, right = pl.pallas_call(
        functools.partial(chain_kernel, nx, nz, chain_plan()),
        out_shape=(
            pltpu.VMEM((feat, d), F32),
            pltpu.VMEM((feat, 128), BF16),
            pltpu.VMEM((RANK, d), F32),
        ),
        in_specs=[any_spec] * 4,
        out_specs=(vmem_spec,) * 3,
        scratch_shapes=[
            pltpu.VMEM((tokens, feat), BF16),
            pltpu.VMEM((feat, tokens), BF16),
            pltpu.VMEM((tokens, d), BF16),
            pltpu.VMEM((feat, d), BF16),
            pltpu.VMEM((RANK, d), F32),
            pltpu.VMEM((2 * RANK, d), BF16),
            pltpu.VMEM((2, NY, RANK, tok), F32),
            pltpu.VMEM((feat, 2 * RANK), F32),
            pltpu.VMEM((nx, RANK // 2, feat), BF16),
            pltpu.VMEM((nz, RANK // 2, feat), BF16),
            pltpu.VMEM((nz, RANK // 2, feat), BF16),
            pltpu.VMEM((nx, RANK // 2, feat), BF16),
            pltpu.VMEM((RANK, feat), F32),
            pltpu.VMEM((2 * RANK, feat), BF16),
            pltpu.VMEM((2, NY, RANK + 8, tok), F32),
            pltpu.VMEM((NY, RANK + 8, tok), F32),
            pltpu.VMEM((NY, RANK + 8, tok), F32),
            pltpu.VMEM((RANK, tok), F32),
            pltpu.VMEM((RANK, tok), F32),
            pltpu.VMEM((2 * RANK, tok), BF16),
            pltpu.VMEM((RANK, 128), F32),
            pltpu.VMEM((RANK, d), F32),
            pltpu.VMEM((RANK, half), F32),
            pltpu.VMEM((nx * nz,) + piece, F32),
            pltpu.VMEM((NY,) + piece, F32),
            pltpu.VMEM((RANK, d), F32),
            dma((4,)),
            dma((2 * CHUNKS,)),
            dma((2 * CHUNKS,)),
            dma((3 * CHUNKS,)),
            dma,
            dma((NT,)),
            dma((nx + nz,)),
            dma((nx + nz,)),
            dma,
            dma((NY,)),
            dma,
            dma,
            dma((nx * nz,)),
            dma((NY,)),
            dma((nx * nz,)),
            dma,
            dma((22,)),
            pltpu.SemaphoreType.REGULAR((6,)),
            pltpu.SemaphoreType.REGULAR,
        ],
        compiler_params=pltpu.CompilerParams(
            collective_id=0, has_side_effects=True, vmem_limit_bytes=VMEM_LIMIT
        ),
        name="gather_and_factors",
    )(activations, out_grads, feedback[0], right_basis.T)
    width = min(512, d // 2)
    vmem = functools.partial(pltpu.with_memory_space_constraint, memory_space=pltpu.VMEM)
    new_feedback, new_right = pl.pallas_call(
        update_kernel,
        out_shape=(
            jax.ShapeDtypeStruct((feat, d), BF16),
            jax.ShapeDtypeStruct((RANK, d), F32),
        ),
        in_specs=[vmem_spec] * 3,
        out_specs=(any_spec, any_spec),
        scratch_shapes=[
            pltpu.VMEM((d // width, feat, width), BF16),
            pltpu.VMEM((128, width), BF16),
            dma((d // width,)),
            dma,
        ],
        compiler_params=pltpu.CompilerParams(vmem_limit_bytes=16 << 20),
        name="update",
    )(vmem(merged), vmem(p3), vmem(right))
    return new_feedback[None], new_right.T


VMEM_LIMIT = 40 << 20


def solution(mesh):
    nx = nz = 4
    in_specs = (P("dp", "tensor"), P(("dp", "tensor"), None), P("dp", "tensor", None), P())
    out_specs = (P("dp", "tensor", None), P())
    return jax.shard_map(
        functools.partial(body, nx, nz), mesh=mesh, in_specs=in_specs, out_specs=out_specs, check_vma=False
    )
```

```python
import functools

import jax
import jax.numpy as jnp
from jax import lax
from jax.experimental import pallas as pl
from jax.experimental.pallas import tpu as pltpu
from jax.sharding import PartitionSpec as P

MESH = pl.DeviceIdType.MESH
F32 = jnp.float32
BF16 = jnp.bfloat16
HIGHEST = lax.Precision.HIGHEST
RANK = 32
AHEAD = 4
NY = 4
NT = 8
WIDTHS = (512,) * 11 + (256, 256)
STARTS = tuple(sum(WIDTHS[:k]) for k in range(len(WIDTHS)))
CHUNKS = len(WIDTHS)
ROWS_FIRST = (((1,), (0,)), ((), ()))
ROWS_BOTH = (((1,), (1,)), ((), ()))


def dot(a, b, dims=ROWS_FIRST, precision=None):
    return lax.dot_general(a, b, dims, precision=precision, preferred_element_type=F32)


def split2(x):
    high = x.astype(BF16)
    low = (x - high.astype(F32)).astype(BF16)
    return high, low


def split3(x):
    high, low = split2(x)
    return high, low, (x - high.astype(F32) - low.astype(F32)).astype(BF16)


def inverse_factor(gram):
    row = lax.broadcasted_iota(jnp.int32, (RANK, 128), 0)
    lane = lax.broadcasted_iota(jnp.int32, (RANK, 128), 1)
    work = jnp.where(lane < RANK, gram, jnp.where(lane == row + RANK, 1.0, 0.0))
    for k in range(RANK):
        column = jnp.broadcast_to(work[:, k : k + 1], (RANK, 128))
        pivot = column[k : k + 1, :]
        inv = lax.rsqrt(pivot)
        inv = inv * (1.5 - 0.5 * pivot * inv * inv)
        scaled = work[k : k + 1, :] * inv
        factor = jnp.where(row > k, column * inv, 0.0)
        work = jnp.where(row == k, scaled, work - factor * scaled)
    return work[:, RANK : 2 * RANK]


def chain_kernel(
    nx, nz, plan,
    a_hbm, g_hbm, f_hbm, q_hbm,
    merged, p3, z_out, linv_out,
    a_v, at_v, g_v, f_v, q_v, q2_v, gq_s, fq_v,
    la1, lb1, la2, lb2, left_v, left2_v,
    al_send, al_sib, al_s, al_fwd, al_in, al2_v, linv_v,
    z_v, zsib, rs_s, y_s, zf,
    load_sem, dir_r, rel_r, sib_r, own_r, gq_r, l1_r, l2_r, als_r, al_r, ali_r, zs_r, rs_r, y_r, ag_r, zf_r, send_sem, round_sem, ring_sem,
):
    tok, d = g_hbm.shape
    feat = f_hbm.shape[0]
    half = d // 2
    piece_r, piece_c = RANK // nx, half // nz
    zw = min(512, d)
    hw = min(512, half)
    hr = RANK // 2
    dp, t = lax.axis_index("dp"), lax.axis_index("tensor")
    x, z = dp // nz, dp % nz
    y, c = t // 2, t % 2
    yp, ym, y2 = (y + 1) % NY, (y + 3) % NY, (y + 2) % NY
    sib = (dp, y * 2 + 1 - c)
    mine, other = c * half, (1 - c) * half
    my_half = pl.ds(pl.multiple_of(mine, 128), half)
    sib_half = pl.ds(pl.multiple_of(other, 128), half)
    dp_peers = [(((x + i) % nx), ((z + k) % nz)) for i in range(nx) for k in range(nz) if i or k]
    x_peers = [((x + i) % nx) for i in range(1, nx)]
    z_peers = [((z + i) % nz) for i in range(1, nz)]
    outgoing = []

    def at_y(yy):
        return (dp, yy * 2 + c)

    def rows(tt, first=0, count=None):
        return pl.ds(pl.multiple_of(tt * tok + first, 16), tok if count is None else count)

    def cols(j):
        return pl.ds(STARTS[j], WIDTHS[j])

    def remote(src, dst, send, recv, device):
        return pltpu.make_async_remote_copy(
            src_ref=src, dst_ref=dst, send_sem=send, recv_sem=recv, device_id=device, device_id_type=MESH
        )

    def send(src, dst, sem, recv, device):
        remote(src, dst, send_sem.at[sem], recv, device).start()
        outgoing.append(sem)

    def receive(ref, recv):
        remote(ref, ref, send_sem.at[0], recv, sib).wait_recv()

    def piece(xx, zz):
        return (
            pl.ds(pl.multiple_of((xx + NY - y) % nx * piece_r, 8), piece_r),
            pl.ds(pl.multiple_of(mine + zz * piece_c, 128), piece_c),
        )

    def total(slots, n):
        out = slots[0].astype(F32)
        for k in range(1, n):
            out = out + slots[k].astype(F32)
        return out

    loads = [
        pltpu.make_async_copy(g_hbm, g_v.at[rows(t), :], load_sem.at[0]),
        pltpu.make_async_copy(q_hbm, q_v, load_sem.at[1]),
        pltpu.make_async_copy(f_hbm, f_v, load_sem.at[2]),
        pltpu.make_async_copy(a_hbm, a_v, load_sem.at[3]),
    ]

    before = [(x > 0, (dp - nz, t)), (z > 0, (dp - 1, t))]
    after = [(x < nx - 1, (dp + nz, t)), (z < nz - 1, (dp + 1, t))]
    ring = [at_y(yp), at_y(ym)]

    def signal(sem, devices):
        for there, device in devices:

            @pl.when(there)
            def _():
                pl.semaphore_signal(sem, 1, device_id=device, device_id_type=MESH)

    def count(devices):
        return sum(there.astype(jnp.int32) for there, _ in devices)

    def enter():
        loads[0].start()
        loads[1].start()
        barrier = pltpu.get_barrier_semaphore()
        for device in ring + [sib]:
            pl.semaphore_signal(barrier, 1, device_id=device, device_id_type=MESH)
        signal(barrier, after)
        loads[0].wait()
        loads[2].start()
        loads[3].start()
        pl.semaphore_wait(barrier, 3 + count(before))
        for device in ring:
            pl.semaphore_signal(ring_sem, 1, device_id=device, device_id_type=MESH)

    def hear_ring():
        pl.semaphore_wait(ring_sem, 2)

    def tell(k):
        signal(round_sem.at[k], before + after if k else before)

    def hear(k):
        told = count(before + after if k else after)

        @pl.when(told > 0)
        def _():
            pl.semaphore_wait(round_sem.at[k], told)

    def wait_load(k):
        loads[k].wait()


    def own():
        send(g_v.at[rows(t), :], g_v.at[rows(t), :], 0, own_r, sib)

    def direct(j):
        block = g_v.at[rows(t), cols(j)]
        send(block, block, 1, dir_r.at[2 * j], at_y(yp))
        send(block, block, 2, dir_r.at[2 * j + 1], at_y(ym))

    def to_sib(tt, j, k):
        block = g_v.at[rows(tt), cols(j)]
        send(block, block, 3 + k, sib_r.at[3 * j + k], sib)

    def relay(j):
        receive(g_v.at[rows(ym * 2 + c), cols(j)], dir_r.at[2 * j])
        block = g_v.at[rows(ym * 2 + c, 0, tok // 2), cols(j)]
        send(block, block, 6, rel_r.at[2 * j], at_y(yp))
        receive(g_v.at[rows(yp * 2 + c), cols(j)], dir_r.at[2 * j + 1])
        block = g_v.at[rows(yp * 2 + c, tok // 2, tok // 2), cols(j)]
        send(block, block, 7, rel_r.at[2 * j + 1], at_y(ym))

    def cross(j):
        to_sib(ym * 2 + c, j, 0)
        to_sib(yp * 2 + c, j, 1)

    def opposite(j):
        receive(g_v.at[rows(y2 * 2 + c, 0, tok // 2), cols(j)], rel_r.at[2 * j])
        receive(g_v.at[rows(y2 * 2 + c, tok // 2, tok // 2), cols(j)], rel_r.at[2 * j + 1])
        to_sib(y2 * 2 + c, j, 2)

    def pump(j, ahead=True):
        relay(j)
        if ahead and j + AHEAD < CHUNKS:
            direct(j + AHEAD)
        cross(j)

    def absorb(j, part=None):
        if j == 0 and part != 1:
            receive(g_v.at[rows(sib[1]), :], own_r)
        for k, yy in enumerate((ym, yp, y2)):
            if part is None or (part == 1) == (k == 2):
                receive(g_v.at[rows(yy * 2 + 1 - c), cols(j)], sib_r.at[3 * j + k])

    def merge(j, part=None):
        absorb(j, part)
        width = min(256, WIDTHS[j])

        def chips(at, *ys):
            out = None
            for yy in ys:
                pair = pl.ds(pl.multiple_of(yy * 2 * tok, 2 * tok), 2 * tok)
                term = dot(at_v[:, pair], g_v[pair, at])
                out = term if out is None else out + term
            return out

        def step(i, carry):
            at = pl.ds(pl.multiple_of(STARTS[j] + i * width, 128), width)
            if part is None:
                merged[:, at] = dot(at_v[...], g_v[:, at]) + f_v[:, at].astype(F32)
            elif part == 0:
                merged[:, at] = chips(at, y, yp, ym) + f_v[:, at].astype(F32)
            else:
                merged[:, at] += chips(at, y2)
            return carry

        lax.fori_loop(0, WIDTHS[j] // width, step, 0)


    y_peers = (yp, y2, ym)

    def project():
        loads[1].wait()
        q2_v[...] = jnp.concatenate(split2(q_v[...]), axis=0)
        gq2 = dot(q2_v[...], g_v[rows(t), :], ROWS_BOTH)
        gq_s[c, y] = gq2[:RANK] + gq2[RANK:]

    def project_send():
        for yy in y_peers:
            send(gq_s.at[c, y], gq_s.at[c, y], 8, gq_r.at[y], at_y(yy))
        send(gq_s.at[c, y], gq_s.at[c, y], 19, gq_r.at[NY + y], sib)

    def project_cross():
        for yy in y_peers:
            receive(gq_s.at[c, yy], gq_r.at[yy])
            send(gq_s.at[c, yy], gq_s.at[c, yy], 19, gq_r.at[NY + yy], sib)

    def carried():
        wait_load(2)
        depth = d // 3
        for k in range(d // depth):
            at = pl.ds(k * depth, depth)
            part = dot(f_v[:, at], q2_v[:, at], ROWS_BOTH)
            if k == 0:
                fq_v[...] = part
            else:
                fq_v[...] += part

    def flip():
        wait_load(3)
        for k in range(NT):
            at_v[:, k * tok : (k + 1) * tok] = jnp.transpose(a_v[k * tok : (k + 1) * tok, :])

    def left_start():
        for yy in range(NY):
            receive(gq_s.at[1 - c, yy], gq_r.at[NY + yy])
        gq = jnp.concatenate([gq_s[k % 2, k // 2] for k in range(NT)], axis=1)
        part = dot(jnp.concatenate(split2(gq), axis=0), a_v[...])
        fq = fq_v[...]
        left_part = part[:RANK] + part[RANK:] + jnp.transpose(fq[:, :RANK] + fq[:, RANK:])
        la1[x] = left_part[:hr].astype(BF16)
        lb1[z] = left_part[hr:].astype(BF16)
        left_send(la1, lb1, l1_r, 9)

    def left_send(slots_x, slots_z, sems, at):
        for xx in x_peers:
            send(slots_x.at[x], slots_x.at[x], at, sems.at[x], (xx * nz + z, t))
        for zz in z_peers:
            send(slots_z.at[z], slots_z.at[z], at + 1, sems.at[nx + z], (x * nz + zz, t))

    def left_receive(slots_x, slots_z, sems):
        for xx in x_peers:
            receive(slots_x.at[xx], sems.at[xx])
        for zz in z_peers:
            receive(slots_z.at[zz], sems.at[nx + zz])

    def left_second():
        left_receive(la1, lb1, l1_r)
        la2[z] = total(la1, nx).astype(BF16)
        lb2[x] = total(lb1, nz).astype(BF16)
        left_send(lb2, la2, l2_r, 11)

    def left_end():
        left_receive(lb2, la2, l2_r)
        left_v[:hr] = total(la2, nz)
        left_v[hr:] = total(lb2, nx)
        left2_v[...] = jnp.concatenate(split2(left_v[...]), axis=0)

    def mapped():
        left = left_v[...]
        al = dot(left2_v[...], at_v[...])
        al = al[:RANK] + al[RANK:]
        gram = dot(left, left, ROWS_BOTH, HIGHEST)
        gram = jnp.concatenate([gram[8 * k : 8 * k + 8] for k in range(RANK // 8)], axis=1)
        for k in range(NT):
            al_send[k % 2, k // 2, :RANK] = al[:, k * tok : (k + 1) * tok]
            al_send[k % 2, k // 2, RANK:] = gram
        send(al_send.at[1 - c], al_sib, 20, als_r, sib)

    def mapped_send():
        receive(al_sib, als_r)
        al_send[c] += al_sib[...]
        for yy in y_peers:
            send(al_send.at[c, yy], al_s.at[y], 13, al_r.at[y], (((x + 1) % nx) * nz + z, yy * 2 + c))

    def mapped_relay():
        for yy in y_peers:
            receive(al_s.at[yy], al_r.at[yy])
        al_s[y] = al_send[c, y]
        fwd = al_s[yp, :RANK] + al_s[y2, :RANK] + al_s[ym, :RANK]
        al_fwd[...] = fwd
        send(al_fwd, al_in, 21, ali_r, (((x + nx - 1) % nx) * nz + z, t))
        gram = total(al_s, NY)[RANK:]
        gram = jnp.concatenate([gram[:, RANK * k : RANK * (k + 1)] for k in range(RANK // 8)], axis=0)
        linv_v[...] = jnp.concatenate([gram, jnp.zeros((RANK, 128 - RANK), F32)], axis=1)

    def z_first():
        def step(i, carry):
            at = pl.ds(pl.multiple_of(i * zw, 128), zw)
            r = dot(left2_v[...], f_v[:, at])
            z_v[:, at] = r[:RANK] + r[RANK:]
            return carry

        lax.fori_loop(0, d // zw, step, 0)

    def mapped_end():
        receive(al_in, ali_r)
        al2_v[...] = jnp.concatenate(split2(al_send[c, y, :RANK] + al_in[...]), axis=0)

    def z_second(base):
        def step(i, carry):
            at = pl.ds(pl.multiple_of(base + i * hw, 128), hw)
            r = dot(al2_v[...], g_v[rows(t), at])
            z_v[:, at] += r[:RANK] + r[RANK:]
            return carry

        lax.fori_loop(0, half // hw, step, 0)

    def z_send():
        z_second(other)
        send(z_v.at[:, sib_half], zsib, 14, zs_r, sib)
        z_second(mine)

    def z_scatter():
        receive(zsib, zs_r)
        z_v[:, my_half] += zsib[...]
        for xx, zz in dp_peers:
            send(z_v.at[piece(xx, zz)], rs_s.at[dp], 15, rs_r.at[dp], (xx * nz + zz, t))
        rs_s[dp] = z_v[piece(x, z)]

    def factor():
        linv = inverse_factor(linv_v[...])
        linv_v[:, :RANK] = linv
        p_high, p_low = split2(dot(linv, left_v[...], precision=HIGHEST))
        p_rows = jnp.concatenate([p_high, p_high, p_low, jnp.zeros((RANK, feat), BF16)], axis=0)
        p3[...] = jnp.transpose(p_rows.astype(F32)).astype(BF16)

    def z_over_y():
        for xx, zz in dp_peers:
            receive(rs_s.at[xx * nz + zz], rs_r.at[xx * nz + zz])
        y_s[y] = total(rs_s, nx * nz)
        for yy in (yp, y2, ym):
            send(y_s.at[y], y_s.at[y], 16, y_r.at[y], (((x + NY - y + yy) % nx) * nz + z, yy * 2 + c))

    def z_back():
        for yy in (yp, y2, ym):
            receive(y_s.at[yy], y_r.at[yy])
        ours = piece(x, z)
        zf[ours] = total(y_s, NY)
        for xx, zz in dp_peers:
            send(zf.at[ours], zf.at[ours], 17, ag_r.at[dp], (xx * nz + zz, t))
        send(zf.at[ours], zf.at[ours], 18, zf_r, sib)

    def z_cross():
        for xx, zz in dp_peers:
            theirs = piece(xx, zz)
            receive(zf.at[theirs], ag_r.at[xx * nz + zz])
            send(zf.at[theirs], zf.at[theirs], 18, zf_r, sib)

    def z_end():
        receive(zf.at[:, sib_half], zf_r)

    def finish():
        z_out[...] = zf[...]
        linv_out[...] = linv_v[...]

    def leave():
        gather = [g_v.at[rows(t), :]] * 6 + [g_v.at[rows(t, 0, tok // 2), :]] * 2
        pieces = gather + [gq_s.at[0, pl.ds(0, NY - 1)]]
        for slots in (la1, lb1, lb2, la2):
            pieces.append(slots.at[pl.ds(0, slots.shape[0] - 1)])
        pieces += [al_s.at[pl.ds(0, NY - 1)], zsib, rs_s.at[pl.ds(0, nx * nz - 1)]]
        pieces += [y_s.at[pl.ds(0, NY - 1)], rs_s.at[pl.ds(0, nx * nz - 1)], zsib]
        pieces += [gq_s.at[0], al_sib, al_in]
        for sem, ref in enumerate(pieces):
            if sem in outgoing:
                remote(ref, ref, send_sem.at[sem], own_r, sib).wait_send()

    steps = dict(tell=tell, hear=hear, hear_ring=hear_ring, project_send=project_send, project_cross=project_cross,
        enter=enter, wait_load=wait_load, absorb=absorb, own=own, direct=direct, relay=relay, cross=cross, opposite=opposite, pump=pump, merge=merge,
        project=project, carried=carried, flip=flip, left_start=left_start, left_second=left_second,
        left_end=left_end, mapped=mapped, mapped_send=mapped_send, mapped_relay=mapped_relay, z_first=z_first, mapped_end=mapped_end,
        z_send=z_send, z_scatter=z_scatter, factor=factor, z_over_y=z_over_y, z_back=z_back, z_cross=z_cross,
        z_end=z_end, finish=finish, leave=leave,
    )
    for name, *args in plan:
        steps[name](*args)


def chain_plan():
    return [
        ("enter",), ("direct", 0), ("project",), ("hear_ring",), ("project_send",), ("tell", 0), ("direct", 1),
        ("direct", 2), ("direct", 3), ("hear", 0), ("tell", 1), ("carried",), ("hear", 1), ("tell", 2),
        ("project_cross",), ("flip",), ("hear", 2), ("tell", 3), ("left_start",), ("own",), ("pump", 0),
        ("hear", 3), ("tell", 4), ("pump", 1), ("left_second",), ("hear", 4), ("tell", 5), ("pump", 2),
        ("pump", 3), ("pump", 4), ("left_end",), ("mapped",), ("mapped_send",), ("z_first",), ("opposite", 0),
        ("mapped_relay",), ("pump", 5), ("opposite", 1), ("hear", 5), ("mapped_end",), ("z_send",), ("pump", 6),
        ("opposite", 2), ("z_scatter",), ("factor",), ("pump", 7), ("opposite", 3), ("merge", 0), ("merge", 1),
        ("merge", 2), ("pump", 8), ("opposite", 4), ("z_over_y",), ("pump", 9), ("opposite", 5), ("merge", 3),
        ("merge", 4), ("z_back",), ("pump", 10), ("opposite", 6), ("merge", 5), ("pump", 11), ("opposite", 7),
        ("merge", 6), ("merge", 7), ("pump", 12), ("merge", 8, 0), ("merge", 9, 0), ("z_cross",), ("opposite", 8),
        ("opposite", 9), ("opposite", 10), ("merge", 8, 1), ("merge", 9, 1), ("opposite", 11), ("merge", 10),
        ("z_end",), ("opposite", 12), ("finish",), ("merge", 11), ("merge", 12), ("leave",),
    ]


def update_kernel(replicas, merged, p3, z, linv, out, right_out, stage, r_v, r3_v, sems, right_sem):
    d = merged.shape[1]
    width = stage.shape[2]
    steps = d // width
    l1, l2, l3 = split3(linv[:, :RANK])
    lhs = jnp.concatenate([l1, l1, l2, l1, l2, l3], axis=1)

    def block(i):
        return pl.ds(pl.multiple_of(i * width, 128), width)

    def copy(i):
        return pltpu.make_async_copy(stage.at[i], out.at[:, block(i)], sems.at[i])

    for i in range(steps):
        z1, z2, z3 = split3(z[:, block(i)])
        rhs = jnp.concatenate([z1, z2, z1, z3, z2, z1], axis=0)
        right = dot(lhs, rhs) * (1.0 / replicas)
        r_v[:, block(i)] = right
        r_high, r_low = split2(right)
        r3_v[...] = jnp.concatenate([r_high, r_low, r_high, jnp.zeros((RANK, width), BF16)], axis=0)
        stage[i] = (merged[:, block(i)] - dot(p3[...], r3_v[...])).astype(BF16)
        copy(i).start()
        pltpu.make_async_copy(r_v.at[:, block(i)], right_out.at[:, block(i)], right_sem).start()
    for i in range(steps):
        copy(i).wait()
    pltpu.make_async_copy(r_v, right_out, right_sem).wait()


def body(nx, nz, activations, out_grads, feedback, right_basis):
    tokens, feat = activations.shape
    tok, d = out_grads.shape
    half = d // 2
    piece = (RANK // nx, half // nz)
    any_spec = pl.BlockSpec(memory_space=pl.ANY)
    vmem_spec = pl.BlockSpec(memory_space=pltpu.VMEM)
    dma = pltpu.SemaphoreType.DMA
    merged, p3, z, linv = pl.pallas_call(
        functools.partial(chain_kernel, nx, nz, chain_plan()),
        out_shape=(
            pltpu.VMEM((feat, d), F32),
            pltpu.VMEM((feat, 128), BF16),
            pltpu.VMEM((RANK, d), F32),
            pltpu.VMEM((RANK, 128), F32),
        ),
        in_specs=[any_spec] * 4,
        out_specs=(vmem_spec,) * 4,
        scratch_shapes=[
            pltpu.VMEM((tokens, feat), BF16),
            pltpu.VMEM((feat, tokens), BF16),
            pltpu.VMEM((tokens, d), BF16),
            pltpu.VMEM((feat, d), BF16),
            pltpu.VMEM((RANK, d), F32),
            pltpu.VMEM((2 * RANK, d), BF16),
            pltpu.VMEM((2, NY, RANK, tok), F32),
            pltpu.VMEM((feat, 2 * RANK), F32),
            pltpu.VMEM((nx, RANK // 2, feat), BF16),
            pltpu.VMEM((nz, RANK // 2, feat), BF16),
            pltpu.VMEM((nz, RANK // 2, feat), BF16),
            pltpu.VMEM((nx, RANK // 2, feat), BF16),
            pltpu.VMEM((RANK, feat), F32),
            pltpu.VMEM((2 * RANK, feat), BF16),
            pltpu.VMEM((2, NY, RANK + 8, tok), F32),
            pltpu.VMEM((NY, RANK + 8, tok), F32),
            pltpu.VMEM((NY, RANK + 8, tok), F32),
            pltpu.VMEM((RANK, tok), F32),
            pltpu.VMEM((RANK, tok), F32),
            pltpu.VMEM((2 * RANK, tok), BF16),
            pltpu.VMEM((RANK, 128), F32),
            pltpu.VMEM((RANK, d), F32),
            pltpu.VMEM((RANK, half), F32),
            pltpu.VMEM((nx * nz,) + piece, F32),
            pltpu.VMEM((NY,) + piece, F32),
            pltpu.VMEM((RANK, d), F32),
            dma((4,)),
            dma((2 * CHUNKS,)),
            dma((2 * CHUNKS,)),
            dma((3 * CHUNKS,)),
            dma,
            dma((NT,)),
            dma((nx + nz,)),
            dma((nx + nz,)),
            dma,
            dma((NY,)),
            dma,
            dma,
            dma((nx * nz,)),
            dma((NY,)),
            dma((nx * nz,)),
            dma,
            dma((22,)),
            pltpu.SemaphoreType.REGULAR((6,)),
            pltpu.SemaphoreType.REGULAR,
        ],
        compiler_params=pltpu.CompilerParams(
            collective_id=0, has_side_effects=True, vmem_limit_bytes=VMEM_LIMIT
        ),
        name="gather_and_factors",
    )(activations, out_grads, feedback[0], right_basis.T)
    width = min(512, d // 2)
    vmem = functools.partial(pltpu.with_memory_space_constraint, memory_space=pltpu.VMEM)
    new_feedback, new_right = pl.pallas_call(
        functools.partial(update_kernel, nx * nz),
        out_shape=(
            jax.ShapeDtypeStruct((feat, d), BF16),
            jax.ShapeDtypeStruct((RANK, d), F32),
        ),
        in_specs=[vmem_spec] * 4,
        out_specs=(any_spec, any_spec),
        scratch_shapes=[
            pltpu.VMEM((d // width, feat, width), BF16),
            pltpu.VMEM((RANK, d), F32),
            pltpu.VMEM((128, width), BF16),
            dma((d // width,)),
            dma,
        ],
        compiler_params=pltpu.CompilerParams(vmem_limit_bytes=16 << 20),
        name="update",
    )(vmem(merged), vmem(p3), vmem(z), vmem(linv))
    return new_feedback[None], new_right.T


VMEM_LIMIT = 40 << 20


def solution(mesh):
    nx = nz = 4
    in_specs = (P("dp", "tensor"), P(("dp", "tensor"), None), P("dp", "tensor", None), P())
    out_specs = (P("dp", "tensor", None), P())
    return jax.shard_map(
        functools.partial(body, nx, nz), mesh=mesh, in_specs=in_specs, out_specs=out_specs, check_vma=False
    )
```
